128 devices in a mesh: seq: 32 (over z, x, core), head: 4 (over y).
Axes of the slice: x: 4, y: 4, z: 4, core: 2. Of those that a mesh axis runs over, the one named last changes fastest.
Arguments:
- tokens: bfloat16 [8192, 1024], P('seq'), may hold values from -6 to 6
- first_gain: bfloat16 [1024], replicated, may hold values from 0.5 to 1.5
- query_weight: bfloat16 [1024, 512], P(None, 'head'), may hold values from -0.1875 to 0.1875
- key_weight: bfloat16 [1024, 512], P(None, 'head'), may hold values from -0.1875 to 0.1875
- value_weight: bfloat16 [1024, 1024], P(None, 'head'), may hold values from -0.1875 to 0.1875
- outgate_weight: bfloat16 [1024, 1024], P(None, 'head'), may hold values from -0.1875 to 0.1875
- decay_down: bfloat16 [1024, 16], replicated, may hold values from -0.1875 to 0.1875
- decay_up: bfloat16 [16, 512], P(None, 'head'), may hold values from -1.5 to 1.5
- decay_bias: bfloat16 [512], P('head'), may hold values from -1 to 9
- head_gain: bfloat16 [256], replicated, may hold values from 0.5 to 1.5
- output_weight: bfloat16 [1024, 1024], P('head'), may hold values from -0.1875 to 0.1875
- second_gain: bfloat16 [1024], replicated, may hold values from 0.5 to 1.5
- mlp_gate: bfloat16 [1024, 2816], P(None, 'head'), may hold values from -0.1875 to 0.1875
- mlp_up: bfloat16 [1024, 2816], P(None, 'head'), may hold values from -0.1875 to 0.1875
- mlp_down: bfloat16 [2816, 1024], P('head'), may hold values from -0.109375 to 0.109375
- cotangent: bfloat16 [8192, 1024], P('seq'), may hold values from -6 to 6
Outputs:
- output: float32 [8192, 1024], P('seq')
- grad_tokens: float32 [8192, 1024], P('seq')
- grad_first_gain: float32 [1024], P('seq')
- grad_query_weight: float32 [1024, 512], P('seq', 'head')
- grad_key_weight: float32 [1024, 512], P('seq', 'head')
- grad_value_weight: float32 [1024, 1024], P('seq', 'head')
- grad_outgate_weight: float32 [1024, 1024], P('seq', 'head')
- grad_decay_down: float32 [1024, 16], P('seq')
- grad_decay_up: float32 [16, 512], P(None, 'head')
- grad_decay_bias: float32 [512], P('head')
- grad_head_gain: float32 [256], P('seq')
- grad_output_weight: float32 [1024, 1024], P('head', 'seq')
- grad_second_gain: float32 [1024], P('seq')
- grad_mlp_gate: float32 [1024, 2816], P('seq', 'head')
- grad_mlp_up: float32 [1024, 2816], P('seq', 'head')
- grad_mlp_down: float32 [2816, 1024], P('head', 'seq')
The draws below stay inside these ranges and needn't reach their ends.
All inputs are finite; a program needn't handle non-finite values.
Results may differ from the reference program's by a relative error of at most 0.012.
The reference program's roundings to bfloat16 on the way count: a program that leaves them out, or rounds other values in their place, can miss the bound.
Values sent between devices are 32-bit elements; how exact they have to be, the bound alone decides.
No kernel may reach another device: no remote copies, remote signals or barrier semaphores. Data moves between devices by JAX's collectives and lax.ppermute only.
A program may use at most 128 MiB of HBM per device.

```python
import jax
import jax.numpy as jnp
from jax import lax

D = 1024
HEAD_K = 128
HEAD_V = 256
RANK = 16
FF = 2816
GROUP = 64
TOKENS = 8192
KEYS = 512
VALUES = 1024


def levels(rng, shape, split, least, high):
    def one(position, parts):
        steps = jax.random.uniform(jax.random.fold_in(jax.random.fold_in(rng, 6), position), (parts,), jnp.float32, least / len(split), high / len(split))
        return jnp.repeat(jnp.exp(steps), shape[position] // parts).reshape((-1,) + (1,) * (len(shape) - position - 1))

    loudness = one(*split[0])
    for cut in split[1:]:
        loudness = loudness * one(*cut)
    return loudness


def scatter_about(stream_key, extent, deviation, most, cuts=(), dtype=jnp.bfloat16):
    drawn = jax.random.normal(stream_key, extent, jnp.float32) * deviation
    if len(cuts) > 0:
        drawn = levels(stream_key, extent, cuts, -0.22, 0.18) * drawn
    return jnp.clip(drawn, min=-most, max=most).astype(dtype)


def setup_inputs(seed: int = 0) -> dict:
    key_list = jax.random.split(jax.random.key(seed), 17)
    tokens = scatter_about(key_list[0], (TOKENS, D), 1.0, 6.0, ((0, 32),))
    first_gain = jnp.clip(1.0 + 0.1 * jax.random.normal(key_list[1], (D,), jnp.float32), 0.5, 1.5).astype(jnp.bfloat16)
    query_weight = scatter_about(key_list[2], (D, KEYS), D ** -0.5, 0.1875, ((1, 4),))
    key_weight = scatter_about(key_list[3], (D, KEYS), D ** -0.5, 0.1875, ((1, 4),))
    value_weight = scatter_about(key_list[4], (D, VALUES), D ** -0.5, 0.1875, ((1, 4),))
    outgate_weight = scatter_about(key_list[5], (D, VALUES), D ** -0.5, 0.1875, ((1, 4),))
    decay_down = scatter_about(key_list[6], (D, RANK), D ** -0.5, 0.1875)
    decay_up = scatter_about(key_list[7], (RANK, KEYS), RANK ** -0.5, 1.5, ((1, 4),))
    decay_bias = jnp.clip(-1.0 + 10.0 * jax.random.uniform(key_list[8], (KEYS,), jnp.float32) ** levels(key_list[8], (KEYS,), ((0, 4),), -0.2, 0.2), -1.0, 9.0).astype(jnp.bfloat16)
    head_gain = jnp.clip(1.0 + 0.1 * jax.random.normal(key_list[9], (HEAD_V,), jnp.float32), 0.5, 1.5).astype(jnp.bfloat16)
    output_weight = scatter_about(key_list[10], (VALUES, D), VALUES ** -0.5, 0.1875, ((0, 4),))
    second_gain = jnp.clip(1.0 + 0.1 * jax.random.normal(key_list[11], (D,), jnp.float32), 0.5, 1.5).astype(jnp.bfloat16)
    mlp_gate = scatter_about(key_list[12], (D, FF), D ** -0.5, 0.1875, ((1, 4),))
    mlp_up = scatter_about(key_list[13], (D, FF), D ** -0.5, 0.1875, ((1, 4),))
    mlp_down = scatter_about(key_list[14], (FF, D), FF ** -0.5, 0.109375, ((0, 4),))
    cotangent = scatter_about(key_list[15], (TOKENS, D), 1.0, 6.0, ((0, 32),))
    return dict(tokens=tokens, first_gain=first_gain, query_weight=query_weight, key_weight=key_weight, value_weight=value_weight, outgate_weight=outgate_weight, decay_down=decay_down, decay_up=decay_up, decay_bias=decay_bias, head_gain=head_gain, output_weight=output_weight, second_gain=second_gain, mlp_gate=mlp_gate, mlp_up=mlp_up, mlp_down=mlp_down, cotangent=cotangent)


epsilon = 1e-05
decay_norm = 16.0
highest = lax.Precision.HIGHEST

@jax.custom_vjp
def low(v):
    return lax.optimization_barrier(v.astype(jnp.bfloat16)).astype(jnp.float32)

@jax.custom_vjp
def low_back(v):
    return v

def low_keep(v):
    return (low(v), None)

def low_pass(kept, grad):
    return (grad,)

def back_keep(v):
    return (v, None)

def back_low(kept, grad):
    return (low(grad),)
low.defvjp(low_keep, low_pass)
low_back.defvjp(back_keep, back_low)

def matmul_high(left, right):
    return jnp.dot(left, right, precision=highest)

def rms_scale(array):
    return lax.rsqrt(lax.optimization_barrier(jnp.mean(array * array, axis=-1, keepdims=True)) + epsilon)

def head_view(array, col_width):
    return array.reshape(array.shape[0], -1, col_width)

def to_blocks(array, col_width):
    block_count = array.shape[0] // GROUP
    return array.reshape(block_count, GROUP, -1, col_width).transpose(0, 2, 1, 3)

def from_blocks(array):
    block_count, head_count, block_len, col_width = array.shape
    return array.transpose(0, 2, 1, 3).reshape(block_count * block_len, head_count * col_width)

def group_step(state_in, pieces):
    query_rows, key_rows, value_rows, log_decay = pieces
    key_scale = query_rows.shape[-1] ** (-0.5)
    cumulative = jnp.cumsum(log_decay, axis=1)
    block_len = query_rows.shape[1]
    row_ids = lax.broadcasted_iota(jnp.int32, (block_len, block_len), 0)
    col_ids = lax.broadcasted_iota(jnp.int32, (block_len, block_len), 1)
    causal = (row_ids >= col_ids)[None, :, :, None]
    spread = cumulative[:, :, None, :] - cumulative[:, None, :, :]
    pair_weight = jnp.where(causal, jnp.exp(jnp.where(causal, spread, 0.0)), 0.0)
    scores = lax.optimization_barrier(jnp.sum(query_rows[:, :, None, :] * key_rows[:, None, :, :] * pair_weight, axis=-1)) * key_scale
    inner_part = jnp.einsum('hij,hjd->hid', scores, value_rows, precision=highest)
    outer_part = jnp.einsum('hic,hcd->hid', query_rows * jnp.exp(cumulative) * key_scale, state_in, precision=highest)
    last_decay = cumulative[:, -1:, :]
    carried = jnp.einsum('hjc,hjd->hcd', key_rows * jnp.exp(last_decay - cumulative), value_rows, precision=highest)
    new_state = jnp.exp(last_decay[:, 0, :])[:, :, None] * state_in + carried
    return (new_state, inner_part + outer_part)

def gla_sequence(query_rows, key_rows, value_rows, log_decay):
    blocks = (to_blocks(query_rows, HEAD_K), to_blocks(key_rows, HEAD_K), to_blocks(value_rows, HEAD_V), to_blocks(log_decay, HEAD_K))
    head_count = query_rows.shape[1] // HEAD_K
    start_state = jnp.zeros((head_count, HEAD_K, HEAD_V), jnp.float32)
    unused_state, mixed_blocks = lax.scan(jax.checkpoint(group_step), start_state, blocks)
    return from_blocks(mixed_blocks)

def forward(token_rows, first_gain, query_weight, key_weight, value_weight, outgate_weight, decay_down, decay_up, decay_bias, head_gain, output_weight, second_gain, mlp_gate, mlp_up, mlp_down):
    normed_one = low(token_rows * rms_scale(token_rows) * first_gain)
    query_rows = low_back(matmul_high(normed_one, query_weight))
    key_rows = low_back(matmul_high(normed_one, key_weight))
    value_rows = low_back(matmul_high(normed_one, value_weight))
    outgate_rows = low_back(matmul_high(normed_one, outgate_weight))
    decay_logit = matmul_high(matmul_high(normed_one, decay_down), decay_up) + decay_bias
    log_decay = jax.nn.log_sigmoid(decay_logit) / decay_norm
    mixed_rows = gla_sequence(query_rows, key_rows, value_rows, log_decay)
    mixed_heads = head_view(mixed_rows, HEAD_V)
    unit_mix = mixed_heads * rms_scale(mixed_heads)
    swish_gate = jax.nn.silu(head_view(outgate_rows, HEAD_V))
    gated_heads = low((unit_mix * head_gain * swish_gate).reshape(mixed_rows.shape))
    middle = token_rows + low_back(matmul_high(gated_heads, output_weight))
    normed_two = low(middle * rms_scale(middle) * second_gain)
    gate_act = low_back(matmul_high(normed_two, mlp_gate))
    up_act = low_back(matmul_high(normed_two, mlp_up))
    hidden = low(jax.nn.silu(gate_act) * up_act)
    return middle + matmul_high(hidden, mlp_down)

def reference(tokens, first_gain, query_weight, key_weight, value_weight, outgate_weight, decay_down, decay_up, decay_bias, head_gain, output_weight, second_gain, mlp_gate, mlp_up, mlp_down, cotangent):
    params = tuple((array.astype(jnp.float32) for array in (tokens, first_gain, query_weight, key_weight, value_weight, outgate_weight, decay_down, decay_up, decay_bias, head_gain, output_weight, second_gain, mlp_gate, mlp_up, mlp_down)))
    output, pullback = jax.vjp(forward, *params)
    grads = pullback(cotangent.astype(jnp.float32))
    return (output, grads[0], grads[1], grads[2], grads[3], grads[4], grads[5], grads[6], grads[7], grads[8], grads[9], grads[10], grads[11], grads[12], grads[13], grads[14])
```

```python
import functools

import jax
import jax.numpy as jnp
from jax import lax
from jax.experimental import pallas as pl
from jax.experimental.pallas import tpu as pltpu
from jax.sharding import PartitionSpec as P

HEAD_K = 128
HEAD_V = 256
epsilon = 1e-05
decay_norm = 16.0
key_scale = HEAD_K ** (-0.5)
f32 = jnp.float32
bf16 = jnp.bfloat16
highest = lax.Precision.HIGHEST

NN = (((1,), (0,)), ((), ()))
NT = (((1,), (1,)), ((), ()))
TN = (((0,), (0,)), ((), ()))


def mm(a, b, dims=NN):
    return lax.dot_general(a, b, dims, preferred_element_type=f32)


def mmh(a, b, dims=NN):
    return lax.dot_general(a, b, dims, precision=highest, preferred_element_type=f32)


def shape(*dims, dtype=f32):
    return jax.ShapeDtypeStruct(dims, dtype)


def kernel_call(body, outs, name, flops, scalars=1, limit=8, scratch=(), far=()):
    def run(*args):
        specs = []
        for i, a in enumerate(args):
            if i < scalars:
                specs.append(pl.BlockSpec(memory_space=pltpu.SMEM))
            elif i in far:
                zeros = (0,) * a.ndim
                specs.append(
                    pl.BlockSpec(a.shape, lambda _, z=zeros: z, pipeline_mode=pl.Buffered(1))
                )
            else:
                specs.append(pl.BlockSpec(memory_space=pltpu.VMEM))
        moved = sum(a.size * a.dtype.itemsize for a in args)
        moved += sum(o.size * o.dtype.itemsize for o in outs)
        return pl.pallas_call(
            body,
            grid=(1,) if far else (),
            out_shape=outs,
            in_specs=specs,
            out_specs=[pl.BlockSpec(memory_space=pltpu.VMEM)] * len(outs),
            scratch_shapes=[pltpu.VMEM(dims, f32) for dims in scratch],
            name=name,
            compiler_params=pltpu.CompilerParams(vmem_limit_bytes=limit * 1024 * 1024),
            cost_estimate=pl.CostEstimate(flops=flops, bytes_accessed=moved, transcendentals=0),
        )(*args)

    return run


def after(value, *earlier):
    return lax.optimization_barrier((value, earlier))[0]


def pieces(array):
    one = array.astype(bf16)
    rest = array - one.astype(f32)
    two = rest.astype(bf16)
    return one, two, (rest - two.astype(f32)).astype(bf16)


def mm_exact(left, right, dims=NN):
    count = right.shape[1]
    out = mm(left, jnp.concatenate(pieces(right), axis=1), dims)
    return out[:, 0:count] + out[:, count : 2 * count] + out[:, 2 * count :]


def rms_scale(array):
    return lax.rsqrt(jnp.mean(array * array, axis=-1, keepdims=True) + epsilon)


def norm_back(grad_normed, unit_rows, gain_row, factor):
    scaled = grad_normed * gain_row
    return factor * (scaled - unit_rows * jnp.mean(scaled * unit_rows, axis=-1, keepdims=True))


def logistic(v):
    return 1.0 / (1.0 + jnp.exp(-v))


def pair_ids(rows):
    return (
        lax.broadcasted_iota(jnp.int32, (rows, rows), 0),
        lax.broadcasted_iota(jnp.int32, (rows, rows), 1),
    )


def level_steps(rows):
    return [1 << k for k in range(rows.bit_length() - 1)]


def odd_rows(step, rows):
    return (lax.broadcasted_iota(jnp.int32, (rows, 1), 0) & step) != 0


def level_maps(rows):
    row_ids, col_ids = pair_ids(rows)
    apart = row_ids ^ col_ids
    lower = jnp.where(col_ids <= row_ids, apart, 2 * rows)
    upper = jnp.where(col_ids > row_ids, apart, 2 * rows)
    return lower, upper


def level_weight(step, decay_parts, maps):
    lower, upper = maps
    near = jnp.where(odd_rows(step, lower.shape[0]), lower, upper)
    picked = jnp.where(near < step, 1.0, 0.0).astype(bf16)
    count = decay_parts.shape[1] // 3
    out = mm(picked, decay_parts)
    return jnp.exp(out[:, 0:count] + out[:, count : 2 * count] + out[:, 2 * count :])


def level_mask(step, maps):
    return jnp.logical_and(maps[0] >= step, maps[0] < 2 * step)


def first_body(
    ids, tokens, gain, key_w, value_w, down, up, bias,
    normed_o, key_o, value_o, decay_o, keep_o, send_o,
):
    rows = tokens[...].astype(f32)
    normed = (rows * rms_scale(rows) * gain[...].astype(f32)).astype(bf16)
    normed_o[...] = normed
    key = mm(normed, key_w[...])
    value = mm(normed, value_w[...])
    logit = mmh(mm(normed, down[...], NT), up[...].astype(f32)) + bias[...].astype(f32)
    decay = (jnp.minimum(logit, 0.0) - jnp.log1p(jnp.exp(-jnp.abs(logit)))) / decay_norm
    key_o[...] = key
    value_o[...] = value
    decay_o[...] = decay
    state = mmh(value, key * tail_weight(decay), TN)
    pack_state(ids[1], state, jnp.sum(decay, axis=0, keepdims=True), keep_o, send_o)


def tail_weight(decay):
    row_ids, col_ids = pair_ids(decay.shape[0])
    return jnp.exp(mm_exact(jnp.where(col_ids > row_ids, 1.0, 0.0).astype(bf16), decay))


def pack_state(core, state, total, keep_o, send_o):
    half = HEAD_V // 2
    first = core == 0
    keep_o[0:half, :] = jnp.where(first, state[0:half], state[half:])
    send_o[0:half, :] = jnp.where(first, state[half:], state[0:half])
    packed = jnp.broadcast_to(total, (8, HEAD_K))
    keep_o[half:, :] = packed
    send_o[half:, :] = packed


def inner_body(
    normed_r, key_r, value_r, decay_r, query_w, gate_w, down, up, bias,
    query_o, gate_o, score_o, inner_o, qexp_o, grown_o, tail_o, keyt_o, state_o, low_o, slope_o,
):
    normed = normed_r[...]
    query = mm(normed, query_w[...])
    gate_o[...] = mm(normed, gate_w[...])
    query_o[...] = query
    key, value, decay = key_r[...], value_r[...], decay_r[...]
    low = mm(normed, down[...], NT)
    low_o[...] = low
    logit = mmh(low, up[...].astype(f32)) + bias[...].astype(f32)
    slope_o[...] = logistic(-logit) / decay_norm
    tail = tail_weight(decay)
    tail_o[...] = tail
    key_tail = key * tail
    keyt_o[...] = key_tail
    state_o[...] = mmh(value, key_tail, TN)
    rows = query.shape[0]
    row_ids, col_ids = pair_ids(rows)
    picked = jnp.where(row_ids >= col_ids, 1.0, 0.0).astype(bf16)
    grown = jnp.exp(mm_exact(picked, decay)) * key_scale
    grown_o[...] = grown
    qexp_o[...] = query * grown
    half = rows // 2
    maps = level_maps(half)
    for at in (0, half):
        cut_q, cut_k, cut_d = (a[at : at + half] for a in (query, key, decay))
        parts = jnp.concatenate(pieces(cut_d), axis=1)
        score = jnp.where(maps[0] == 0, jnp.sum(cut_q * cut_k, axis=-1, keepdims=True), 0.0)
        for step in level_steps(half):
            weight = level_weight(step, parts, maps)
            odd = odd_rows(step, half)
            left = jnp.where(odd, cut_q * weight, 0.0)
            right = jnp.where(odd, 0.0, cut_k * weight)
            score = jnp.where(level_mask(step, maps), mmh(left, right, NT), score)
        score_o[at : at + half, at : at + half] = score * key_scale
    score_o[0:half, half:] = jnp.zeros((half, half), f32)
    left, right = half_weights(decay)
    score_o[half:, 0:half] = mmh(query[half:] * left, key[:half] * right, NT) * key_scale
    inner_o[...] = mmh(score_o[...], value)


def half_weights(decay):
    half = decay.shape[0] // 2
    row_ids, col_ids = pair_ids(half)
    upto = jnp.where(row_ids >= col_ids, 1.0, 0.0).astype(bf16)
    beyond = jnp.where(row_ids < col_ids, 1.0, 0.0).astype(bf16)
    return jnp.exp(mm_exact(upto, decay[half:])), jnp.exp(mm_exact(beyond, decay[:half]))


def heads_body(ids, own, mine1, mine2, mine3, other1, other2, other3, out):
    half = mine1.shape[0]
    low = ids[1] == 0
    out[0] = own[...]
    for i, (mine, other) in enumerate(((mine1, other1), (mine2, other2), (mine3, other3))):
        out[i + 1, 0:half, :] = jnp.where(low, mine[...], other[...]).astype(bf16)
        out[i + 1, half:, :] = jnp.where(low, other[...], mine[...]).astype(bf16)


def join_halves(core, mine, theirs):
    first = core == 0
    return jnp.concatenate(
        [jnp.where(first, mine, theirs), jnp.where(first, theirs, mine)], axis=0
    )


def gated_body(ids, inner, qexp, mine, theirs, gate, gain, mixed_o, gated_o, start_o):
    start = join_halves(ids[1], mine[...], theirs[...])
    start_o[...] = start
    mixed = inner[...] + mmh(qexp[...], start, NT)
    mixed_o[...] = mixed
    unit = mixed * rms_scale(mixed)
    gate_rows = gate[...]
    swish = gate_rows * logistic(gate_rows)
    gated_o[...] = (unit * gain[...].astype(f32) * swish).astype(bf16).astype(f32)


def split_rows(head, array, outs):
    count = array.shape[0] // 4
    for i, out in enumerate(outs):
        place = lax.rem(head + i, 4)
        out[...] = array[pl.ds(pl.multiple_of(place * count, count), count), :]


def feed_body(
    ids, tokens, gated0, gated1, gated2, gated3, out_w, gain, gate_w, up_w, grad_hidden,
    middle_o, normed_o, hidden_o, ggate_o, gup_o, part0, part1, part2, part3, total,
):
    middle = tokens[...].astype(f32)
    for i, gated in enumerate((gated0, gated1, gated2, gated3)):
        middle = middle + mm(gated[...].astype(bf16), out_w[i])
    middle_o[...] = middle
    normed = (middle * rms_scale(middle) * gain[...].astype(f32)).astype(bf16)
    normed_o[...] = normed
    gate = mm(normed, gate_w[...], NT)
    up = mm(normed, up_w[...], NT)
    sig = logistic(gate)
    swish = gate * sig
    hidden_o[...] = (swish * up).astype(bf16)
    grad = grad_hidden[...]
    grad_gate = (grad * up * (sig * (1.0 + gate * (1.0 - sig)))).astype(bf16)
    grad_up = (grad * swish).astype(bf16)
    ggate_o[...] = grad_gate
    gup_o[...] = grad_up
    total[...] = mm(grad_gate, gate_w[...]) + mm(grad_up, up_w[...])
    split_rows(ids[0], total, (part0, part1, part2, part3))


def middle_body(
    ids, middle, cot, gain, out_w, part0, part1, part2, part3,
    grad_o, sum_o, gated0, gated1, gated2, gated3,
):
    count = part0.shape[0]
    place = pl.ds(pl.multiple_of(ids[0] * count, count), count)
    rows = middle[place, :]
    factor = rms_scale(rows)
    unit = rows * factor
    grad = part0[...] + part1[...] + part2[...] + part3[...]
    sum_o[...] = jnp.sum(grad * unit, axis=0, keepdims=True)
    grad_middle = cot[place, :].astype(f32) + norm_back(grad, unit, gain[...].astype(f32), factor)
    grad_o[...] = grad_middle
    low = grad_middle.astype(bf16)
    for i, out in enumerate((gated0, gated1, gated2, gated3)):
        out[...] = mm(low, out_w[i], NT)


def mixed_body(
    ids, part0, part1, part2, part3, mixed_r, gate_r, gain_r, qexp, decay,
    gmix_o, gout_o, sum_o, keep_o, send_o, total,
):
    count = part0.shape[0]
    for i, part in enumerate((part0, part1, part2, part3)):
        place = lax.rem(ids[0] + i, 4)
        total[pl.ds(pl.multiple_of(place * count, count), count), :] = part[...]
    grad = total[...]
    mixed = mixed_r[...]
    factor = rms_scale(mixed)
    unit = mixed * factor
    gain = gain_r[...].astype(f32)
    gate = gate_r[...]
    sig = logistic(gate)
    swish = gate * sig
    slope = sig * (1.0 + gate * (1.0 - sig))
    gout_o[...] = (grad * unit * gain * slope).astype(bf16)
    inward = grad * swish
    sum_o[...] = jnp.sum(inward * unit, axis=0, keepdims=True)
    gmix = norm_back(inward, unit, gain, factor)
    gmix_o[...] = gmix
    state = mmh(gmix, qexp[...], TN)
    pack_state(ids[1], state, jnp.sum(decay[...], axis=0, keepdims=True), keep_o, send_o)


def inner_back_body(
    gmix_r, query_r, key_r, value_r, decay_r, score, grown, start, gout, gate_w, query_w,
    gquery_o, both_o, gkey_o, gvalue_o, early_o,
):
    gmix = gmix_r[...]
    query, key, decay = query_r[...], key_r[...], decay_r[...]
    rows = query.shape[0]
    pair = mmh(gmix, value_r[...], NT) * key_scale
    gvalue_o[...] = mmh(score[...], gmix, TN)
    half = rows // 2
    maps = level_maps(half)
    left, right = half_weights(decay)
    low_pair = pair[half:, 0:half]
    far_q = left * mmh(low_pair, key[:half] * right)
    far_k = right * mmh(low_pair, query[half:] * left, TN)
    from_start = grown[...] * mmh(gmix, start[...])
    all_q, all_k = [], []
    for at in (0, half):
        cut_q, cut_k, cut_d = (a[at : at + half] for a in (query, key, decay))
        cut_pair = pair[at : at + half, at : at + half]
        parts = jnp.concatenate(pieces(cut_d), axis=1)
        same = jnp.sum(jnp.where(maps[0] == 0, cut_pair, 0.0), axis=-1, keepdims=True)
        gq, gk = same * cut_k, same * cut_q
        for step in level_steps(half):
            weight = level_weight(step, parts, maps)
            odd = odd_rows(step, half)
            left = jnp.where(odd, cut_q * weight, 0.0)
            right = jnp.where(odd, 0.0, cut_k * weight)
            inside = jnp.where(level_mask(step, maps), cut_pair, 0.0)
            gq = gq + weight * mmh(inside, right)
            gk = gk + weight * mmh(inside, left, TN)
        all_q.append(gq)
        all_k.append(gk)
    gquery = from_start + jnp.concatenate([all_q[0], all_q[1] + far_q], axis=0)
    gkey = jnp.concatenate([all_k[0] + far_k, all_k[1]], axis=0)
    both_o[...] = query * gquery
    low = gquery.astype(bf16)
    gquery_o[...] = low
    gkey_o[...] = gkey
    early_o[...] = mm(gout[...], gate_w[...], NT) + mm(low, query_w[...], NT)


def outer_back_body(
    ids, mine, theirs, start, state, key_r, value_r, decay_r, tail, key_tail, both, gkey_r, gvalue_r,
    slope, low, early, key_w, value_w, up, down, tokens,
    gkey_o, gvalue_o, glow_o, small_o, sum_o, part0, part1, part2, part3, total,
):
    end = join_halves(ids[1], mine[...], theirs[...])
    key = key_r[...]
    gkey = gkey_r[...] + tail[...] * mmh(value_r[...], end)
    gvalue = gvalue_r[...] + mmh(key_tail[...], end, NT)
    whole = jnp.exp(jnp.sum(decay_r[...], axis=0, keepdims=True))
    later = jnp.sum((whole * start[...] + state[...]) * end, axis=0, keepdims=True)
    row_ids, col_ids = pair_ids(key.shape[0])
    picked = jnp.where(col_ids >= row_ids, 1.0, 0.0).astype(bf16)
    gdecay = mm_exact(picked, both[...] - key * gkey) + later
    glogit = gdecay * slope[...]
    glow = mmh(glogit, up[...].astype(f32), NT)
    glow_o[...] = glow
    small_o[0:16, :] = mmh(low[...], glogit, TN)
    small_o[16:24, :] = jnp.broadcast_to(jnp.sum(glogit, axis=0, keepdims=True), (8, HEAD_K))
    gkey_low = gkey.astype(bf16)
    gvalue_low = gvalue.astype(bf16)
    gkey_o[...] = gkey_low
    gvalue_o[...] = gvalue_low
    grad = early[...] + mm(gkey_low, key_w[...], NT) + mm(gvalue_low, value_w[...], NT)
    grad = grad + mmh(glow, down[...].astype(f32))
    rows = tokens[...].astype(f32)
    sum_o[...] = jnp.sum(grad * (rows * rms_scale(rows)), axis=0, keepdims=True)
    total[...] = grad
    split_rows(ids[0], total, (part0, part1, part2, part3))


def last_body(ids, tokens, gain, grad_middle, part0, part1, part2, part3, out):
    count = part0.shape[0]
    rows = tokens[pl.ds(pl.multiple_of(ids[0] * count, count), count), :].astype(f32)
    factor = rms_scale(rows)
    grad = part0[...] + part1[...] + part2[...] + part3[...]
    out[...] = grad_middle[...] + norm_back(grad, rows * factor, gain[...].astype(f32), factor)


def join_body(ids, part0, part1, part2, part3, out):
    count = part0.shape[0]
    for i, part in enumerate((part0, part1, part2, part3)):
        place = lax.rem(ids[0] + 4 - i, 4)
        out[pl.ds(pl.multiple_of(place * count, count), count), :] = part[...]


def weights_one_body(normed, cot, hidden, grad_gate, grad_up, keep_o, send_o):
    half = keep_o.shape[0]
    width = grad_gate.shape[1]
    for out, at in ((keep_o, 0), (send_o, half)):
        left = normed[:, at : at + half]
        out[:, 0:width] = mm(left, grad_gate[...], TN)
        out[:, width : 2 * width] = mm(left, grad_up[...], TN)
        tail = jnp.zeros((half, out.shape[1] - 3 * width), f32)
        down = mm(cot[:, at : at + half], hidden[...], TN)
        out[:, 2 * width :] = jnp.concatenate([down, tail], axis=1)


def weights_two_body(
    normed, gquery, gkey, gvalue, gout, low, gated, glow, select, source, first_sum, second_sum,
    head_sum, keep_o, send_o,
):
    half = keep_o.shape[0]
    width = select.shape[0]
    glow_parts = jnp.concatenate(pieces(glow[...]), axis=1)
    rank = glow.shape[1]
    rows = jnp.concatenate([first_sum[...], second_sum[...], jnp.zeros((6, width), f32)], axis=0)
    row_parts = jnp.concatenate(pieces(rows), axis=0)
    heads = jnp.concatenate(
        [jnp.zeros((2, HEAD_V), f32), head_sum[...], jnp.zeros((5, HEAD_V), f32)], axis=0
    )
    head_parts = jnp.concatenate(pieces(heads), axis=0)
    share = HEAD_V // 32
    for out, at in ((keep_o, 0), (send_o, half)):
        left = normed[:, at : at + half]
        out[:, 0:128] = mm(left, gquery[...], TN)
        out[:, 128:256] = mm(left, gkey[...], TN)
        out[:, 256:512] = mm(left, gvalue[...], TN)
        out[:, 512:768] = mm(left, gout[...], TN)
        out[:, 768:1024] = mm(low[:, at : at + half], gated[...].astype(bf16), TN)
        down = mm(left, glow_parts, TN)
        from_feature = source[:, at : at + half]
        inside = from_feature & 31
        from_head = jnp.where(inside < share, (from_feature >> 5) * share + inside, -1)
        head_ids = lax.broadcasted_iota(jnp.int32, (HEAD_V, half), 0)
        spread = jnp.where(head_ids == from_head, 1.0, 0.0).astype(bf16)
        tail = mm(select[:, at : at + half], row_parts, (((0,), (1,)), ((), ())))
        tail = tail + mm(spread, head_parts, (((0,), (1,)), ((), ())))
        out[:, 1024:1152] = jnp.concatenate(
            [
                down[:, 0:rank] + down[:, rank : 2 * rank] + down[:, 2 * rank :],
                tail[:, 0:8] + tail[:, 8:16] + tail[:, 16:24],
                jnp.zeros((half, 104), f32),
            ],
            axis=1,
        )


def cut(packed):
    half = HEAD_V // 2
    return packed[0:half, :], packed[half : half + 1, :]


def pack(out, state, decay):
    half = HEAD_V // 2
    out[0:half, :] = state
    out[half:, :] = jnp.broadcast_to(decay, (8, HEAD_K))


def chip_body(reverse, ids, keep, other, first_o, chip_o):
    mine, theirs = keep[...], other[...]
    is_first = ids[1] == (1 if reverse else 0)
    first = jnp.where(is_first, mine, theirs)
    first_o[...] = first
    first_state, first_decay = cut(first)
    second_state, second_decay = cut(jnp.where(is_first, theirs, mine))
    pack(
        chip_o, jnp.exp(second_decay) * first_state + second_state, first_decay + second_decay
    )


def earlier(parts, place):
    state, decay = 0.0, jnp.zeros((1, HEAD_K), f32)
    for d in (1, 2, 3):
        part_state, part_decay = cut(parts[d - 1])
        held = place >= d
        state = state + jnp.where(held, jnp.exp(decay), 0.0) * part_state
        decay = decay + jnp.where(held, part_decay, 0.0)
    return state, decay


def line_body(reverse, ids, own, part1, part2, part3, row_o, whole_o):
    line = 3 - ids[2] if reverse else ids[2]
    parts = [own[...], part1[...], part2[...], part3[...]]
    pack(row_o, *earlier(parts[1:], line))
    whole = 0.0
    for d in range(4):
        decay = jnp.zeros((1, HEAD_K), f32)
        for e in range(4):
            if e != d:
                later = lax.rem(line + 4 - e, 4) > lax.rem(line + 4 - d, 4)
                decay = decay + jnp.where(later, cut(parts[e])[1], 0.0)
        whole = whole + jnp.exp(decay) * cut(parts[d])[0]
    pack(whole_o, whole, sum(cut(p)[1] for p in parts))


def plane_body(reverse, ids, part1, part2, part3, row, first, mine_o, theirs_o):
    deep = 3 - ids[3] if reverse else ids[3]
    plane_state, _ = earlier([part1[...], part2[...], part3[...]], deep)
    row_state, row_decay = cut(row[...])
    before = jnp.exp(row_decay) * plane_state + row_state
    first_state, first_decay = cut(first[...])
    past = jnp.exp(first_decay) * before + first_state
    is_first = ids[1] == (1 if reverse else 0)
    mine_o[...] = jnp.where(is_first, before, past)
    theirs_o[...] = jnp.where(is_first, past, before)


def scan_states(ids, keep, send, reverse, beside):
    sign = -1 if reverse else 1
    side = "later" if reverse else "earlier"
    packed = [shape(HEAD_V // 2 + 8, HEAD_K)] * 2
    other = swap_core(send)
    first, chip = kernel_call(
        functools.partial(chip_body, reverse), packed, "chip_" + side, 0, limit=2
    )(ids, keep, other)
    row, whole = kernel_call(
        functools.partial(line_body, reverse), packed, "line_" + side, 0, limit=2
    )(ids, chip, *[move_x(chip, sign * d) for d in (1, 2, 3)])
    row = after(row, beside)
    mine, theirs = kernel_call(
        functools.partial(plane_body, reverse),
        [shape(HEAD_V // 2, HEAD_K)] * 2,
        "plane_" + side,
        0,
        limit=2,
    )(ids, *[move_z(whole, sign * d) for d in (1, 2, 3)], row, first)
    return (mine, swap_core(theirs)), chip


def part_body(keep, other, *outs):
    kept = keep.shape[0] // 2
    size = kept // 4
    for side in (0, 1):
        own, one, two_up, two_down, three = outs[5 * side : 5 * side + 5]
        for out, at in (
            (own, 0), (one, size), (two_up, 2 * size), (two_down, 5 * size // 2), (three, 3 * size)
        ):
            rows = slice(side * kept + at, side * kept + at + out.shape[0])
            out[...] = keep[rows, :] + other[rows, :]


def relay_body(one_a, three_a, up_a, down_a, one_b, three_b, up_b, down_b, *outs):
    half = up_a.shape[0]
    for at, (one, three, up, down) in enumerate(
        ((one_a, three_a, up_a, down_a), (one_b, three_b, up_b, down_b))
    ):
        to_one, to_three = outs[2 * at : 2 * at + 2]
        to_one[0:half, :] = one[0:half, :] + up[...]
        to_one[half:, :] = one[half:, :]
        to_three[0:half, :] = three[0:half, :]
        to_three[half:, :] = three[half:, :] + down[...]


def fine_body(own_a, up_a, down_a, own_b, up_b, down_b, *outs):
    size = outs[0].shape[0]
    for side, (own, up, down) in enumerate(((own_a, up_a, down_a), (own_b, up_b, down_b))):
        for d in range(4):
            rows = slice(d * size, (d + 1) * size)
            outs[4 * side + d][...] = own[rows, :] + up[rows, :] + down[rows, :]


def turned(array):
    count = array.shape[0]
    row_ids, col_ids = pair_ids(count)
    same = jnp.where(row_ids == col_ids, 1.0, 0.0)
    return mmh(array, same, TN)


def end_body(cuts, a0, a1, a2, a3, b0, b1, b2, b3, *outs):
    rows = jnp.concatenate(
        [
            a0[...] + a1[...] + a2[...] + a3[...],
            b0[...] + b1[...] + b2[...] + b3[...],
        ],
        axis=0,
    )
    for out, (low, high) in zip(outs, cuts):
        out[...] = rows[:, low:high]


def tiny_body(part0, part1, part2, part3, down_o, first_o, second_o, head_o):
    rows = turned(part0[...] + part1[...] + part2[...] + part3[...])
    rank = down_o.shape[0]
    down_o[...] = rows[0:rank]
    for i, out in enumerate((first_o, second_o, head_o)):
        out[...] = rows[rank + i : rank + i + 1, 0 : out.shape[1]]


def start_scatter(keep, send, name):
    kept, cols = keep.shape[0] // 2, keep.shape[1]
    size = kept // 4
    sizes = [size, size, size // 2, size // 2, size]
    other = swap_core(send)
    return kernel_call(
        part_body, [shape(n, cols) for n in sizes * 2], name + "_part", 0, scalars=0, limit=12
    )(keep, other)


def end_scatter(parts, name, cuts):
    own_a, one_a, up_a, down_a, three_a, own_b, one_b, up_b, down_b, three_b = parts
    size, cols = own_a.shape
    one_a, three_a, one_b, three_b = kernel_call(
        relay_body, [shape(size, cols)] * 4, name + "_relay", 0, scalars=0, limit=12
    )(
        one_a, three_a, move_x(up_a, 1), move_x(down_a, -1),
        one_b, three_b, move_z(up_b, 1), move_z(down_b, -1),
    )
    fine = kernel_call(
        fine_body, [shape(size // 4, cols)] * 8, name + "_fine", 0, scalars=0, limit=12
    )(
        own_a, move_x(one_a, 1), move_x(three_a, -1), own_b, move_z(one_b, 1), move_z(three_b, -1)
    )
    outs = [shape(size // 2, high - low) for low, high in cuts]
    return kernel_call(
        functools.partial(end_body, cuts), outs, name + "_end", 0, scalars=0, limit=8
    )(
        fine[0], *[move_z(fine[d], d) for d in (1, 2, 3)],
        fine[4], *[move_x(fine[4 + d], d) for d in (1, 2, 3)],
    )


def seq_pairs(move):
    pairs = []
    for source in range(32):
        z, x, core = source // 8, (source // 2) % 4, source % 2
        z, x, core = move(z, x, core)
        pairs.append((source, ((z % 4) * 4 + x % 4) * 2 + core % 2))
    return pairs


def swap_core(array):
    return lax.ppermute(array, "seq", seq_pairs(lambda z, x, c: (z, x, c + 1)))


def move_x(array, d):
    return lax.ppermute(array, "seq", seq_pairs(lambda z, x, c: (z, x + d, c)))


def move_z(array, d):
    return lax.ppermute(array, "seq", seq_pairs(lambda z, x, c: (z + d, x, c)))


def move_y(array, d):
    return lax.ppermute(array, "head", [(s, (s + d) % 4) for s in range(4)])


def sum_seq(array):
    array = array + swap_core(array)
    array = array + move_x(array, 1) + move_x(array, 2) + move_x(array, 3)
    return array + move_z(array, 1) + move_z(array, 2) + move_z(array, 3)


def gather_y(array):
    return [array] + [move_y(array, d) for d in (1, 2, 3)]


def on_device(
    tokens,
    first_gain,
    query_weight,
    key_weight,
    value_weight,
    outgate_weight,
    decay_down,
    decay_up,
    decay_bias,
    head_gain,
    output_weight,
    second_gain,
    mlp_gate,
    mlp_up,
    mlp_down,
    cotangent,
):
    place = lax.axis_index("seq")
    head = lax.axis_index("head")
    z, x, core = place // 8, (place // 2) % 4, place % 2
    ids = jnp.stack([head, core, x, z]).astype(jnp.int32)
    rows, width = tokens.shape
    quarter = rows // 4
    hidden_width = mlp_gate.shape[1]
    first_row = first_gain.reshape(1, -1)
    second_row = second_gain.reshape(1, -1)
    head_row = head_gain.reshape(1, -1)

    packed = [shape(HEAD_V // 2 + 8, HEAD_K)] * 2
    bias_row = decay_bias.reshape(1, -1)
    normed_one, key, value, decay, keep, send = kernel_call(
        first_body,
        [
            shape(rows, width, dtype=bf16),
            shape(rows, HEAD_K),
            shape(rows, HEAD_V),
            shape(rows, HEAD_K),
        ]
        + packed,
        "first",
        400_000_000,
        far=range(1, 8),
    )(ids, tokens, first_row, key_weight, value_weight, decay_down.T, decay_up, bias_row)

    (
        query, outgate, score, inner, query_grown, grown, tail, key_tail, own_state, low_rank, slope,
    ) = kernel_call(
        inner_body,
        [
            shape(rows, HEAD_K),
            shape(rows, HEAD_V),
            shape(rows, rows),
            shape(rows, HEAD_V),
            shape(rows, HEAD_K),
            shape(rows, HEAD_K),
            shape(rows, HEAD_K),
            shape(rows, HEAD_K),
            shape(HEAD_V, HEAD_K),
            shape(rows, decay_down.shape[1]),
            shape(rows, HEAD_K),
        ],
        "inner",
        3_000_000_000,
        scalars=0,
        far=range(4, 9),
    )(
        normed_one, key, value, decay, query_weight, outgate_weight, decay_down.T, decay_up,
        bias_row,
    )
    start_halves, chip = scan_states(ids, keep, send, False, inner)

    half = output_weight.shape[0] // 2
    my_half = lax.dynamic_slice_in_dim(output_weight, core * half, half, 0).astype(f32)
    my_half = after(my_half, chip)
    from_heads = [move_y(my_half, d) for d in (1, 2, 3)]
    other_halves = [swap_core(a) for a in from_heads]
    out_weights = kernel_call(
        heads_body, [shape(4, *output_weight.shape, dtype=bf16)], "heads", 0, scalars=1
    )(ids, output_weight, *from_heads, *other_halves)[0]
    order = jnp.arange(width)
    side, one, two = (order >> 8) & 1, (order >> 6) & 3, (order >> 4) & 3
    to_x = (x + jnp.where(side == 0, one, two)) % 4
    to_z = (z + jnp.where(side == 0, two, one)) % 4
    to_core = (core + (order >> 9)) % 2
    source = to_z * 256 + to_x * 64 + to_core * 32 + side * 16 + (order & 15)
    select = (jnp.arange(width)[:, None] == source[None, :]).astype(bf16)
    grad_hidden = mm(cotangent, mlp_down, NT)
    cot_sent = jnp.dot(cotangent, select)
    normed_one_sent = jnp.dot(normed_one, select)

    mixed, gated, start_state = kernel_call(
        gated_body,
        [shape(rows, HEAD_V), shape(rows, HEAD_V), shape(HEAD_V, HEAD_K)],
        "gated",
        100_000_000,
    )(ids, inner, query_grown, *start_halves, outgate, head_row)
    all_gated = gather_y(gated)

    quarters = [shape(quarter, width)] * 4
    wide = [shape(rows, hidden_width, dtype=bf16)] * 3
    (
        middle, normed_two, hidden, grad_gate_act, grad_up_act, *parts,
    ) = kernel_call(
        feed_body,
        [shape(rows, width), shape(rows, width, dtype=bf16)] + wide + quarters,
        "feed",
        2_000_000_000,
        far=(1, 7, 8, 9),
        scratch=[(rows, width)],
        limit=16,
    )(ids, tokens, *all_gated, out_weights, second_row, mlp_gate.T, mlp_up.T, grad_hidden)
    parts = [parts[0]] + [move_y(parts[d], d) for d in (1, 2, 3)]

    normed_two_sent = jnp.dot(normed_two, select)
    keep_one, send_one = kernel_call(
        weights_one_body,
        [shape(width // 2, -(-3 * hidden_width // 128) * 128)] * 2,
        "weights_one",
        1_200_000_000,
        scalars=0,
    )(normed_two_sent, cot_sent, hidden, grad_gate_act, grad_up_act)
    parts_one = start_scatter(keep_one, send_one, "one")
    parts[0] = after(parts[0], keep_one)
    ffn_part = jnp.dot(hidden, mlp_down, preferred_element_type=f32)

    grad_middle, second_sum, *grad_heads = kernel_call(
        middle_body,
        [shape(quarter, width), shape(1, width)] + [shape(quarter, HEAD_V)] * 4,
        "middle",
        200_000_000,
        far=(2, 3),
    )(ids, middle, cotangent, second_row, out_weights, *parts)
    grad_heads = [grad_heads[0]] + [move_y(grad_heads[d], -d) for d in (1, 2, 3)]
    grad_heads[0] = after(grad_heads[0], parts_one)

    grad_mixed, grad_outgate, head_sum, keep, send = kernel_call(
        mixed_body,
        [
            shape(rows, HEAD_V),
            shape(rows, HEAD_V, dtype=bf16),
            shape(1, HEAD_V),
            shape(HEAD_V // 2 + 8, HEAD_K),
            shape(HEAD_V // 2 + 8, HEAD_K),
        ],
        "mixed",
        100_000_000,
        scratch=[(rows, HEAD_V)],
    )(ids, *grad_heads, mixed, outgate, head_row, query_grown, decay)

    grad_query, both, inner_key, inner_value, early = kernel_call(
        inner_back_body,
        [
            shape(rows, HEAD_K, dtype=bf16),
            shape(rows, HEAD_K),
            shape(rows, HEAD_K),
            shape(rows, HEAD_V),
            shape(rows, width),
        ],
        "inner_back",
        5_000_000_000,
        scalars=0,
        far=(9, 10),
    )(
        grad_mixed, query, key, value, decay, score, grown, start_state, grad_outgate,
        outgate_weight, query_weight,
    )

    end_halves, _ = scan_states(ids, keep, send, True, early)
    ffn_part = after(ffn_part, grad_heads)
    ffn_parts = [
        lax.dynamic_slice_in_dim(ffn_part, ((head + d) % 4) * quarter, quarter, 0) for d in range(4)
    ]
    out_rows = lax.dynamic_slice_in_dim(middle, head * quarter, quarter, 0) + ffn_parts[0]
    for d in (1, 2, 3):
        out_rows = out_rows + move_y(ffn_parts[d], d)
    early = after(early, out_rows)

    grad_key, grad_value, grad_low, small, first_sum, *parts = kernel_call(
        outer_back_body,
        [
            shape(rows, HEAD_K, dtype=bf16),
            shape(rows, HEAD_V, dtype=bf16),
            shape(rows, decay_down.shape[1]),
            shape(24, HEAD_K),
            shape(1, width),
        ]
        + quarters,
        "outer_back",
        1_000_000_000,
        far=range(16, 21),
        scratch=[(rows, width)],
        limit=16,
    )(
        ids, *end_halves, start_state, own_state, key, value, decay, tail, key_tail, both, inner_key,
        inner_value, slope, low_rank, early, key_weight, value_weight, decay_up, decay_down.T, tokens,
    )
    parts_one = [after(p, grad_low) for p in parts_one]
    parts = [parts[0]] + [move_y(parts[d], d) for d in (1, 2, 3)]
    small = sum_seq(after(small, parts))
    out_rows = after(out_rows, parts)

    def join(array, name):
        return kernel_call(join_body, [shape(rows, width)], name, 0, scalars=1)(
            ids, *gather_y(array)
        )[0]

    output = join(out_rows, "join_output")
    grad_middle_all = join(grad_middle, "join_middle")
    grad_low_sent = jnp.dot(grad_middle_all.astype(bf16), select)
    grad_rows = kernel_call(last_body, [shape(quarter, width)], "last", 0, scalars=1)(
        ids, tokens, first_row, grad_middle, *parts
    )[0]
    grad_tokens = join(grad_rows, "join_tokens")

    keep_two, send_two = kernel_call(
        weights_two_body,
        [shape(width // 2, 1152)] * 2,
        "weights_two",
        1_200_000_000,
        scalars=0,
    )(
        normed_one_sent, grad_query, grad_key, grad_value, grad_outgate, grad_low_sent, gated,
        grad_low, select, source[None, :], first_sum, second_sum, head_sum,
    )
    parts_two = start_scatter(keep_two, send_two, "two")
    grad_gate, grad_up, grad_down = end_scatter(
        parts_one,
        "one",
        (
            (0, hidden_width),
            (hidden_width, 2 * hidden_width),
            (2 * hidden_width, 3 * hidden_width),
        ),
    )
    grad_query_w, grad_key_w, grad_value_w, grad_outgate_w, grad_output_w, tiny = end_scatter(
        parts_two,
        "two",
        (
            (0, 128),
            (128, 256),
            (256, 512),
            (512, 768),
            (768, 1024),
            (1024, 1152),
        ),
    )
    grad_down_w, grad_first, grad_second, grad_head = kernel_call(
        tiny_body,
        [shape(decay_down.shape[1], 32), shape(1, 32), shape(1, 32), shape(1, HEAD_V // 32)],
        "tiny",
        0,
        scalars=0,
        limit=2,
    )(*gather_y(tiny))
    return (
        output,
        grad_tokens,
        grad_first[0],
        grad_query_w,
        grad_key_w,
        grad_value_w,
        grad_outgate_w,
        grad_down_w.T,
        small[0:16],
        small[16],
        grad_head[0],
        grad_output_w.T,
        grad_second[0],
        grad_gate,
        grad_up,
        grad_down.T,
    )


def solution(mesh):
    placed = (
        P("seq", None),
        P(),
        P(None, "head"),
        P(None, "head"),
        P(None, "head"),
        P(None, "head"),
        P(),
        P(None, "head"),
        P("head"),
        P(),
        P("head", None),
        P(),
        P(None, "head"),
        P(None, "head"),
        P("head", None),
        P("seq", None),
    )
    return jax.shard_map(
        on_device,
        mesh=mesh,
        in_specs=placed,
        out_specs=(
            P("seq", None),
            P("seq", None),
            P("seq"),
            P("seq", "head"),
            P("seq", "head"),
            P("seq", "head"),
            P("seq", "head"),
            P("seq", None),
            P(None, "head"),
            P("head"),
            P("seq"),
            P("head", "seq"),
            P("seq"),
            P("seq", "head"),
            P("seq", "head"),
            P("head", "seq"),
        ),
        check_vma=False,
    )
```

```python
import functools

import jax
import jax.numpy as jnp
from jax import lax
from jax.experimental import pallas as pl
from jax.experimental.pallas import tpu as pltpu
from jax.sharding import PartitionSpec as P

HEAD_K = 128
HEAD_V = 256
epsilon = 1e-05
decay_norm = 16.0
key_scale = HEAD_K ** (-0.5)
f32 = jnp.float32
bf16 = jnp.bfloat16
highest = lax.Precision.HIGHEST

NN = (((1,), (0,)), ((), ()))
NT = (((1,), (1,)), ((), ()))
TN = (((0,), (0,)), ((), ()))


def mm(a, b, dims=NN):
    return lax.dot_general(a, b, dims, preferred_element_type=f32)


def mmh(a, b, dims=NN):
    return lax.dot_general(a, b, dims, precision=highest, preferred_element_type=f32)


def shape(*dims, dtype=f32):
    return jax.ShapeDtypeStruct(dims, dtype)


def kernel_call(body, outs, name, shade, scalars=1, limit=8, scratch=(), far=(), away=(), late=(), work=1):
    def run(*args):
        count, results = len(args), len(outs)

        def whole(*refs):
            refs = list(refs)
            sems = refs.pop()
            held = refs[count + results + len(scratch) :]
            ins, results_refs = refs[:count], refs[count : count + results]
            copies, writes = [], []
            for i in far:
                copies.append(pltpu.make_async_copy(ins[i], held[len(copies)], sems.at[len(copies)]))
                copies[-1].start()
                ins[i] = held[len(copies) - 1]
            for i in away:
                at = len(far) + len(writes)
                writes.append(pltpu.make_async_copy(held[at], results_refs[i], sems.at[at]))
                results_refs[i] = held[at]
            for i, copy in zip(far, copies):
                if i not in late:
                    copy.wait()
            given = [dict(zip(far, copies))] if late else []
            own = refs[count + results : count + results + len(scratch)]
            body(*given, *ins, *results_refs, *own)
            for write in writes:
                write.start()
            for write in writes:
                write.wait()

        specs = []
        for i in range(count):
            space = pltpu.SMEM if i < scalars else pltpu.HBM if i in far else pltpu.VMEM
            specs.append(pl.BlockSpec(memory_space=space))
        out_specs = [
            pl.BlockSpec(memory_space=pltpu.HBM if i in away else pltpu.VMEM)
            for i in range(results)
        ]
        scratches = [pltpu.VMEM(dims, f32) for dims in scratch]
        scratches += [pltpu.VMEM(args[i].shape, args[i].dtype) for i in far]
        scratches += [pltpu.VMEM(outs[i].shape, outs[i].dtype) for i in away]
        scratches.append(pltpu.SemaphoreType.DMA((max(1, len(far) + len(away)),)))
        args = [
            pltpu.with_memory_space_constraint(a, pltpu.HBM) if i in far else a
            for i, a in enumerate(args)
        ]
        return pl.pallas_call(
            whole,
            out_shape=[
                pltpu.HBM(o.shape, o.dtype) if i in away else o for i, o in enumerate(outs)
            ],
            in_specs=specs,
            out_specs=out_specs,
            scratch_shapes=scratches,
            name=name,
            compiler_params=pltpu.CompilerParams(vmem_limit_bytes=limit * 1024 * 1024),
            cost_estimate=pl.CostEstimate(
                flops=10**13 if shade else work,
                bytes_accessed=sum(a.size * a.dtype.itemsize for a in [*args, *outs]) if shade else 1,
                transcendentals=0,
            ),
        )(*args)

    return run


def after(value, *earlier):
    return lax.optimization_barrier((value, earlier))[0]


def pieces(array):
    one = array.astype(bf16)
    rest = array - one.astype(f32)
    two = rest.astype(bf16)
    return one, two, (rest - two.astype(f32)).astype(bf16)


def mm_exact(left, right, dims=NN):
    count = right.shape[1]
    out = mm(left, jnp.concatenate(pieces(right), axis=1), dims)
    return out[:, 0:count] + out[:, count : 2 * count] + out[:, 2 * count :]


def rms_scale(array):
    return lax.rsqrt(jnp.mean(array * array, axis=-1, keepdims=True) + epsilon)


def norm_back(grad_normed, unit_rows, gain_row, factor):
    scaled = grad_normed * gain_row
    return factor * (scaled - unit_rows * jnp.mean(scaled * unit_rows, axis=-1, keepdims=True))


def logistic(v):
    return 1.0 / (1.0 + jnp.exp(-v))


def pair_ids(rows):
    return (
        lax.broadcasted_iota(jnp.int32, (rows, rows), 0),
        lax.broadcasted_iota(jnp.int32, (rows, rows), 1),
    )


def level_steps(rows):
    return [1 << k for k in range(rows.bit_length() - 1)]


def odd_rows(step, rows):
    return (lax.broadcasted_iota(jnp.int32, (rows, 1), 0) & step) != 0


def level_maps(rows):
    row_ids, col_ids = pair_ids(rows)
    apart = row_ids ^ col_ids
    lower = jnp.where(col_ids <= row_ids, apart, 2 * rows)
    upper = jnp.where(col_ids > row_ids, apart, 2 * rows)
    return lower, upper


def level_weight(step, decay_parts, maps):
    lower, upper = maps
    near = jnp.where(odd_rows(step, lower.shape[0]), lower, upper)
    picked = jnp.where(near < step, 1.0, 0.0).astype(bf16)
    count = decay_parts.shape[1] // 3
    out = mm(picked, decay_parts)
    return jnp.exp(out[:, 0:count] + out[:, count : 2 * count] + out[:, 2 * count :])


def level_mask(step, maps):
    return jnp.logical_and(maps[0] >= step, maps[0] < 2 * step)


def first_body(
    ids, gain, bias, tokens, key_w, value_w, down, up,
    normed_o, rows_o, keep_o, send_o,
):
    rows = tokens[...].astype(f32)
    normed = (rows * rms_scale(rows) * gain[...]).astype(bf16)
    normed_o[...] = normed
    key = mm(normed, key_w[...])
    value = mm(normed, value_w[...])
    logit = mmh(mm(normed, down[...], NT), up[...].astype(f32)) + bias[...]
    decay = (jnp.minimum(logit, 0.0) - jnp.log1p(jnp.exp(-jnp.abs(logit)))) / decay_norm
    rows_o[:, 0:128] = key
    rows_o[:, 128:384] = value
    rows_o[:, 384:512] = decay
    state = mmh(value, key * tail_weight(decay), TN)
    pack_state(ids[1], state, jnp.sum(decay, axis=0, keepdims=True), keep_o, send_o)


def tail_weight(decay):
    row_ids, col_ids = pair_ids(decay.shape[0])
    return jnp.exp(mm_exact(jnp.where(col_ids > row_ids, 1.0, 0.0).astype(bf16), decay))


def pack_state(core, state, total, keep_o, send_o):
    half = HEAD_V // 2
    first = core == 0
    keep_o[0:half, :] = jnp.where(first, state[0:half], state[half:])
    send_o[0:half, :] = jnp.where(first, state[half:], state[0:half])
    packed = jnp.broadcast_to(total, (8, HEAD_K))
    keep_o[half:, :] = packed
    send_o[half:, :] = packed


def split_rows_kvd(rows):
    return rows.at[:, 0:128], rows.at[:, 128:384], rows.at[:, 384:512]


def inner_body(
    bias, normed_r, rows_r, query_w, gate_w, down, up, near_o, kept_o, score_o,
):
    gate_o, inner_o, qexp_o = near_o.at[:, 0:256], near_o.at[:, 256:512], near_o.at[:, 512:640]
    query_o, grown_o, tail_o = (kept_o.at[:, 128 * i : 128 * i + 128] for i in range(3))
    keyt_o, state_o, slope_o, low_o = (kept_o.at[:, 128 * i : 128 * i + 128] for i in range(3, 7))
    key_r, value_r, decay_r = split_rows_kvd(rows_r)
    normed = normed_r[...]
    query = mm(normed, query_w[...])
    gate_o[...] = mm(normed, gate_w[...])
    query_o[...] = query
    key, value, decay = key_r[...], value_r[...], decay_r[...]
    low = mm(normed, down[...], NT)
    low_o[...] = jnp.concatenate([low, jnp.zeros((low.shape[0], 112), f32)], axis=1)
    logit = mmh(low, up[...].astype(f32)) + bias[...]
    slope_o[...] = logistic(-logit) / decay_norm
    tail = tail_weight(decay)
    tail_o[...] = tail
    key_tail = key * tail
    keyt_o[...] = key_tail
    state_o[...] = mmh(value, key_tail, TN)
    rows = query.shape[0]
    row_ids, col_ids = pair_ids(rows)
    picked = jnp.where(row_ids >= col_ids, 1.0, 0.0).astype(bf16)
    grown = jnp.exp(mm_exact(picked, decay)) * key_scale
    grown_o[...] = grown
    qexp_o[...] = query * grown
    half = rows // 2
    maps = level_maps(half)
    for at in (0, half):
        cut_q, cut_k, cut_d = (a[at : at + half] for a in (query, key, decay))
        parts = jnp.concatenate(pieces(cut_d), axis=1)
        score = jnp.where(maps[0] == 0, jnp.sum(cut_q * cut_k, axis=-1, keepdims=True), 0.0)
        for step in level_steps(half):
            weight = level_weight(step, parts, maps)
            odd = odd_rows(step, half)
            left = jnp.where(odd, cut_q * weight, 0.0)
            right = jnp.where(odd, 0.0, cut_k * weight)
            score = jnp.where(level_mask(step, maps), mmh(left, right, NT), score)
        score_o[at : at + half, at : at + half] = score * key_scale
    score_o[0:half, half:] = jnp.zeros((half, half), f32)
    left, right = half_weights(decay)
    score_o[half:, 0:half] = mmh(query[half:] * left, key[:half] * right, NT) * key_scale
    inner_o[...] = mmh(score_o[...], value)


def half_weights(decay):
    half = decay.shape[0] // 2
    row_ids, col_ids = pair_ids(half)
    upto = jnp.where(row_ids >= col_ids, 1.0, 0.0).astype(bf16)
    beyond = jnp.where(row_ids < col_ids, 1.0, 0.0).astype(bf16)
    return jnp.exp(mm_exact(upto, decay[half:])), jnp.exp(mm_exact(beyond, decay[:half]))


def forward_body(one, three, upper, lower):
    half = upper.shape[0]
    upper[...] = one[0:half, :]
    lower[...] = three[half:, :]


def bundle_body(one, upper, lower, three, out):
    half = upper.shape[0]
    out[0] = one[...]
    out[1, 0:half, :] = upper[...]
    out[1, half:, :] = lower[...]
    out[2] = three[...]


def heads_body(ids, own, mine, other, out):
    half = mine.shape[1]
    low = ids[1] == 0
    out[0] = own[...]
    for i in range(3):
        out[i + 1, 0:half, :] = jnp.where(low, mine[i], other[i]).astype(bf16)
        out[i + 1, half:, :] = jnp.where(low, other[i], mine[i]).astype(bf16)


def join_halves(core, mine, theirs):
    first = core == 0
    return jnp.concatenate(
        [jnp.where(first, mine, theirs), jnp.where(first, theirs, mine)], axis=0
    )


def gated_body(ids, gain, near, mine, theirs, mixed_o, gated_o, start_o):
    gate, inner, qexp = near.at[:, 0:256], near.at[:, 256:512], near.at[:, 512:640]
    start = join_halves(ids[1], mine[...], theirs[...])
    start_o[...] = start
    mixed = inner[...] + mmh(qexp[...], start, NT)
    mixed_o[...] = mixed
    unit = mixed * rms_scale(mixed)
    gate_rows = gate[...]
    swish = gate_rows * logistic(gate_rows)
    gated_o[...] = (unit * gain[...] * swish).astype(bf16).astype(f32)


def split_rows(head, array, outs):
    count = array.shape[0] // 4
    for i, out in enumerate(outs):
        place = lax.rem(head + i, 4)
        out[...] = array[pl.ds(pl.multiple_of(place * count, count), count), :]


def feed_body(
    ids, gain, tokens, gated0, gated1, gated2, gated3, out_w, gate_w, up_w, grad_hidden,
    middle_o, normed_o, hidden_o, ggate_o, gup_o, part0, part1, part2, part3, total,
):
    middle = tokens[...].astype(f32)
    for i, gated in enumerate((gated0, gated1, gated2, gated3)):
        middle = middle + mm(gated[...].astype(bf16), out_w[i])
    middle_o[...] = middle
    normed = (middle * rms_scale(middle) * gain[...]).astype(bf16)
    normed_o[...] = normed
    gate = mm(normed, gate_w[...], NT)
    up = mm(normed, up_w[...], NT)
    sig = logistic(gate)
    swish = gate * sig
    hidden_o[...] = (swish * up).astype(bf16)
    grad = grad_hidden[...]
    grad_gate = (grad * up * (sig * (1.0 + gate * (1.0 - sig)))).astype(bf16)
    grad_up = (grad * swish).astype(bf16)
    ggate_o[...] = grad_gate
    gup_o[...] = grad_up
    total[...] = mm(grad_gate, gate_w[...]) + mm(grad_up, up_w[...])
    split_rows(ids[0], total, (part0, part1, part2, part3))


def middle_body(
    ids, gain, middle, cot, out_w, part0, part1, part2, part3,
    grad_o, sum_o, gated0, gated1, gated2, gated3,
):
    count = grad_o.shape[0]
    place = pl.ds(pl.multiple_of(ids[0] * count, count), count)
    rows = middle[place, :]
    factor = rms_scale(rows)
    unit = rows * factor
    grad = part0[...] + part1[...] + part2[...] + part3[...]
    sum_o[...] = jnp.sum(grad * unit, axis=0, keepdims=True)
    grad_middle = cot[place, :].astype(f32) + norm_back(grad, unit, gain[...], factor)
    grad_o[...] = grad_middle
    low = grad_middle.astype(bf16)
    for i, out in enumerate((gated0, gated1, gated2, gated3)):
        out[...] = mm(low, out_w[i], NT)


def sum_quarters(parts):
    count = parts.shape[0] // 4
    return (
        parts[0:count, :]
        + parts[count : 2 * count, :]
        + parts[2 * count : 3 * count, :]
        + parts[3 * count :, :]
    )


def mixed_body(
    ids, gain_r, part0, part1, part2, part3, mixed_r, near, rows,
    gmix_o, gout_o, sum_o, keep_o, send_o, total,
):
    gate_r, qexp = near.at[:, 0:256], near.at[:, 512:640]
    decay = rows.at[:, 384:512]
    count = part0.shape[0]
    for i, part in enumerate((part0, part1, part2, part3)):
        place = lax.rem(ids[0] + i, 4)
        total[pl.ds(pl.multiple_of(place * count, count), count), :] = part[...]
    grad = total[...]
    mixed = mixed_r[...]
    factor = rms_scale(mixed)
    unit = mixed * factor
    gain = gain_r[...]
    gate = gate_r[...]
    sig = logistic(gate)
    swish = gate * sig
    slope = sig * (1.0 + gate * (1.0 - sig))
    gout_o[...] = (grad * unit * gain * slope).astype(bf16)
    inward = grad * swish
    sum_o[...] = jnp.sum(inward * unit, axis=0, keepdims=True)
    gmix = norm_back(inward, unit, gain, factor)
    gmix_o[...] = gmix
    state = mmh(gmix, qexp[...], TN)
    pack_state(ids[1], state, jnp.sum(decay[...], axis=0, keepdims=True), keep_o, send_o)


def inner_back_body(
    gmix_r, rows_r, kept, score, start, gout, gate_w, query_w, gquery_o, back_o, early_o,
):
    query_r, grown = kept.at[:, 0:128], kept.at[:, 128:256]
    key_r, value_r, decay_r = split_rows_kvd(rows_r)
    both_o, gkey_o, gvalue_o = back_o.at[:, 0:128], back_o.at[:, 128:256], back_o.at[:, 256:512]
    gmix = gmix_r[...]
    query, key, decay = query_r[...], key_r[...], decay_r[...]
    rows = query.shape[0]
    pair = mmh(gmix, value_r[...], NT) * key_scale
    gvalue_o[...] = mmh(score[...], gmix, TN)
    half = rows // 2
    maps = level_maps(half)
    left, right = half_weights(decay)
    low_pair = pair[half:, 0:half]
    far_q = left * mmh(low_pair, key[:half] * right)
    far_k = right * mmh(low_pair, query[half:] * left, TN)
    from_start = grown[...] * mmh(gmix, start[...])
    all_q, all_k = [], []
    for at in (0, half):
        cut_q, cut_k, cut_d = (a[at : at + half] for a in (query, key, decay))
        cut_pair = pair[at : at + half, at : at + half]
        parts = jnp.concatenate(pieces(cut_d), axis=1)
        same = jnp.sum(jnp.where(maps[0] == 0, cut_pair, 0.0), axis=-1, keepdims=True)
        gq, gk = same * cut_k, same * cut_q
        for step in level_steps(half):
            weight = level_weight(step, parts, maps)
            odd = odd_rows(step, half)
            left = jnp.where(odd, cut_q * weight, 0.0)
            right = jnp.where(odd, 0.0, cut_k * weight)
            inside = jnp.where(level_mask(step, maps), cut_pair, 0.0)
            gq = gq + weight * mmh(inside, right)
            gk = gk + weight * mmh(inside, left, TN)
        all_q.append(gq)
        all_k.append(gk)
    gquery = from_start + jnp.concatenate([all_q[0], all_q[1] + far_q], axis=0)
    gkey = jnp.concatenate([all_k[0] + far_k, all_k[1]], axis=0)
    both_o[...] = query * gquery
    low = gquery.astype(bf16)
    gquery_o[...] = low
    gkey_o[...] = gkey
    early_o[...] = mm(gout[...], gate_w[...], NT) + mm(low, query_w[...], NT)


def outer_back_body(
    copies, ids, mine, theirs, start, rows_r, kept, back, early, key_w, value_w, up, down, tokens,
    second_sum, head_sum, gkv_o, packet_o, small_o, total,
):
    tail, key_tail, state, slope, low = (
        kept.at[:, 128 * i : 128 * i + 128] for i in range(2, 7)
    )
    key_r, value_r, decay_r = split_rows_kvd(rows_r)
    both, gkey_r, gvalue_r = back.at[:, 0:128], back.at[:, 128:256], back.at[:, 256:512]
    end = join_halves(ids[1], mine[...], theirs[...])
    key = key_r[...]
    gkey = gkey_r[...] + tail[...] * mmh(value_r[...], end)
    gvalue = gvalue_r[...] + mmh(key_tail[...], end, NT)
    whole = jnp.exp(jnp.sum(decay_r[...], axis=0, keepdims=True))
    later = jnp.sum((whole * start[...] + state[...]) * end, axis=0, keepdims=True)
    row_ids, col_ids = pair_ids(key.shape[0])
    picked = jnp.where(col_ids >= row_ids, 1.0, 0.0).astype(bf16)
    gdecay = mm_exact(picked, both[...] - key * gkey) + later
    glogit = gdecay * slope[...]
    glow = mmh(glogit, up[...].astype(f32), NT)
    turned_low = mmh(up[...].astype(f32), glogit, NT)
    for i in range(4):
        packet_o[i : i + 1, :] = jnp.concatenate(
            [turned_low[4 * i + j : 4 * i + j + 1, :] for j in range(4)], axis=1
        )
    small_o[0:16, :] = mmh(low[:, 0:16], glogit, TN)
    small_o[16:24, :] = jnp.broadcast_to(jnp.sum(glogit, axis=0, keepdims=True), (8, HEAD_K))
    gkey_low = gkey.astype(bf16)
    gvalue_low = gvalue.astype(bf16)
    gkv_o[:, 0:128] = gkey_low
    gkv_o[:, 128:384] = gvalue_low
    for i in (7, 8, 9, 11, 12):
        copies[i].wait()
    grad = early[...] + mm(gkey_low, key_w[...], NT) + mm(gvalue_low, value_w[...], NT)
    grad = grad + mmh(glow, down[...].astype(f32))
    rows = tokens[...].astype(f32)
    packet_o[4:5, :] = jnp.sum(grad * (rows * rms_scale(rows)), axis=0, keepdims=True)
    packet_o[5:6, :] = second_sum[...]
    packet_o[6:7, :] = jnp.concatenate(
        [head_sum[...], jnp.zeros((1, rows.shape[1] - HEAD_V), f32)], axis=1
    )
    packet_o[7:8, :] = jnp.zeros((1, rows.shape[1]), f32)
    total[...] = grad


def last_body(ids, gain, tokens, grad_middle, parts, out):
    count = grad_middle.shape[0]
    rows = tokens[pl.ds(pl.multiple_of(ids[0] * count, count), count), :].astype(f32)
    factor = rms_scale(rows)
    grad = parts[0:count, :] + parts[count : 2 * count, :] + parts[2 * count : 3 * count, :]
    grad = grad + parts[3 * count :, :]
    grad = grad_middle[...] + norm_back(grad, rows * factor, gain[...], factor)
    for i in range(4):
        out[i * count : (i + 1) * count, :] = grad


def add_body(left, right, out):
    out[...] = left[...] + right[...]


def weights_one_body(normed, cot, hidden, grad_gate, grad_up, keep_o, send_o):
    half = keep_o.shape[0]
    width = grad_gate.shape[1]
    for out, at in ((keep_o, 0), (send_o, half)):
        left = normed[:, at : at + half]
        out[:, 0:width] = mm(left, grad_gate[...], TN)
        out[:, width : 2 * width] = mm(left, grad_up[...], TN)
        tail = jnp.zeros((half, out.shape[1] - 3 * width), f32)
        down = mm(cot[:, at : at + half], hidden[...], TN)
        out[:, 2 * width :] = jnp.concatenate([down, tail], axis=1)


def weights_two_body(
    normed, gquery, gkv, gout, low, gated, select, source, packet0, packet1, packet2, packet3,
    small, keep_o, send_o,
):
    half = normed.shape[1] // 2
    low_sent = mm(low[...].astype(bf16), select[...]).astype(bf16)
    width = select.shape[0]
    packet = packet0[...] + packet1[...] + packet2[...] + packet3[...]
    count = normed.shape[0]
    turned_low = jnp.concatenate(
        [packet[i // 4 : i // 4 + 1, (i % 4) * count : (i % 4 + 1) * count] for i in range(16)],
        axis=0,
    )
    rank = turned_low.shape[0]
    glow_parts = jnp.concatenate(pieces(turned_low), axis=0)
    rows = jnp.concatenate([packet[4:6, :], jnp.zeros((6, width), f32)], axis=0)
    row_parts = jnp.concatenate(pieces(rows), axis=0)
    heads = jnp.concatenate(
        [jnp.zeros((2, HEAD_V), f32), packet[6:7, 0:HEAD_V], jnp.zeros((5, HEAD_V), f32)], axis=0
    )
    head_parts = jnp.concatenate(pieces(heads), axis=0)
    share = HEAD_V // 32
    for out, at in ((keep_o, 0), (send_o, half)):
        left = normed[:, at : at + half]
        out[half:, :] = jnp.concatenate(
            [small[0:8, :], small[8:16, :], small[16:24, :], jnp.zeros((8, 768), f32)], axis=1
        )
        out[0:half, 0:128] = mm(left, gquery[...], TN)
        out[0:half, 128:256] = mm(left, gkv[:, 0:128], TN)
        out[0:half, 256:512] = mm(left, gkv[:, 128:384], TN)
        out[0:half, 512:768] = mm(left, gout[...], TN)
        out[0:half, 768:1024] = mm(low_sent[:, at : at + half], gated[...].astype(bf16), TN)
        down = mm(left, glow_parts, (((0,), (1,)), ((), ())))
        from_feature = source[:, at : at + half]
        inside = from_feature & 31
        from_head = jnp.where(inside < share, (from_feature >> 5) * share + inside, -1)
        head_ids = lax.broadcasted_iota(jnp.int32, (HEAD_V, half), 0)
        spread = jnp.where(head_ids == from_head, 1.0, 0.0).astype(bf16)
        tail = mm(select[:, at : at + half], row_parts, (((0,), (1,)), ((), ())))
        tail = tail + mm(spread, head_parts, (((0,), (1,)), ((), ())))
        out[0:half, 1024:1152] = jnp.concatenate(
            [
                down[:, 0:rank] + down[:, rank : 2 * rank] + down[:, 2 * rank :],
                tail[:, 0:8] + tail[:, 8:16] + tail[:, 16:24],
                jnp.zeros((half, 104), f32),
            ],
            axis=1,
        )


def cut(packed):
    half = HEAD_V // 2
    return packed[0:half, :], packed[half : half + 1, :]


def pack(out, state, decay):
    half = HEAD_V // 2
    out[0:half, :] = state
    out[half:, :] = jnp.broadcast_to(decay, (8, HEAD_K))


def chip_body(reverse, ids, keep, other, first_o, chip_o):
    mine, theirs = keep[...], other[...]
    is_first = ids[1] == (1 if reverse else 0)
    first = jnp.where(is_first, mine, theirs)
    first_o[...] = first
    first_state, first_decay = cut(first)
    second_state, second_decay = cut(jnp.where(is_first, theirs, mine))
    pack(
        chip_o, jnp.exp(second_decay) * first_state + second_state, first_decay + second_decay
    )


def earlier(parts, place):
    state, decay = 0.0, jnp.zeros((1, HEAD_K), f32)
    for d in (1, 2, 3):
        part_state, part_decay = cut(parts[d - 1])
        held = place >= d
        state = state + jnp.where(held, jnp.exp(decay), 0.0) * part_state
        decay = decay + jnp.where(held, part_decay, 0.0)
    return state, decay


def line_body(reverse, ids, own, part1, part2, part3, row_o, whole_o):
    line = 3 - ids[2] if reverse else ids[2]
    parts = [own[...], part1[...], part2[...], part3[...]]
    pack(row_o, *earlier(parts[1:], line))
    whole = 0.0
    for d in range(4):
        decay = jnp.zeros((1, HEAD_K), f32)
        for e in range(4):
            if e != d:
                later = lax.rem(line + 4 - e, 4) > lax.rem(line + 4 - d, 4)
                decay = decay + jnp.where(later, cut(parts[e])[1], 0.0)
        whole = whole + jnp.exp(decay) * cut(parts[d])[0]
    pack(whole_o, whole, sum(cut(p)[1] for p in parts))


def plane_body(reverse, ids, part1, part2, part3, row, first, mine_o, theirs_o):
    deep = 3 - ids[3] if reverse else ids[3]
    plane_state, _ = earlier([part1[...], part2[...], part3[...]], deep)
    row_state, row_decay = cut(row[...])
    before = jnp.exp(row_decay) * plane_state + row_state
    first_state, first_decay = cut(first[...])
    past = jnp.exp(first_decay) * before + first_state
    is_first = ids[1] == (1 if reverse else 0)
    mine_o[...] = jnp.where(is_first, before, past)
    theirs_o[...] = jnp.where(is_first, past, before)


def scan_states(ids, keep, send, reverse, beside, beside_line=None):
    sign = -1 if reverse else 1
    side = "later" if reverse else "earlier"
    packed = [shape(HEAD_V // 2 + 8, HEAD_K)] * 2
    other = swap_core(send)
    first, chip = kernel_call(
        functools.partial(chip_body, reverse), packed, "chip_" + side, False, limit=2
    )(ids, keep, other)
    from_x = [move_x(chip, sign * d) for d in (1, 2, 3)]
    extra = None
    if beside_line is not None:
        extra = beside_line(from_x[0])
        chip = after(chip, extra)
    row, whole = kernel_call(
        functools.partial(line_body, reverse), packed, "line_" + side, False, limit=2
    )(ids, chip, *from_x)
    extra = (chip, row) if extra is None else extra
    row = after(row, beside)
    mine, theirs = kernel_call(
        functools.partial(plane_body, reverse),
        [shape(HEAD_V // 2, HEAD_K)] * 2,
        "plane_" + side,
        False,
        limit=2,
    )(ids, *[move_z(whole, sign * d) for d in (1, 2, 3)], row, first)
    return (mine, swap_core(theirs)), extra


def part_body(extra, keep, other, own, one, up, down, three, *sums):
    size = own.shape[0]
    half = size // 2
    for out, at in ((own, 0), (one, size), (up, 2 * size), (down, 2 * size + half), (three, 3 * size)):
        count = min(out.shape[0], half) if out is up or out is down else size
        out[0:count, :] = keep[at : at + count, :] + other[at : at + count, :]
    if extra:
        total = keep[4 * size :, :] + other[4 * size :, :]
        up[half:, :] = total
        down[half:, :] = total
        sums[0][...] = total


def relay_body(extra, one, three, up, down, *rest):
    size = three.shape[0]
    half = size // 2
    sums, to_one, to_three = rest[:extra], rest[extra], rest[extra + 1]
    to_one[0:half, :] = one[0:half, :] + up[0:half, :]
    to_one[half:size, :] = one[half:, :]
    to_three[0:half, :] = three[0:half, :]
    to_three[half:, :] = three[half:, :] + down[0:half, :]
    if extra:
        to_one[size:, :] = up[half:, :]
        rest[extra + 2][...] = sums[0][...] + up[half:, :] + down[half:, :]


def fine_body(extra, own, up, down, *rest):
    sums, outs = rest[:extra], rest[extra:]
    count = outs[0].shape[0]
    total = None
    if extra:
        total = sums[0][...] + up[4 * count :, :]
        outs[4][...] = total
    for d in range(4):
        rows = slice(d * count, (d + 1) * count)
        outs[d][0:count, :] = own[rows, :] + up[rows, :] + down[rows, :]
        if extra and d > 0:
            outs[d][count:, :] = total


def turned(array):
    count = array.shape[0]
    row_ids, col_ids = pair_ids(count)
    same = jnp.where(row_ids == col_ids, 1.0, 0.0)
    return mmh(array, same, TN)


def end_body(extra, cuts, part0, part1, part2, part3, *rest):
    sums, outs = rest[:extra], rest[extra:]
    count = part0.shape[0]
    rows = part0[...] + part1[0:count, :] + part2[0:count, :] + part3[0:count, :]
    for out, (low, high) in zip(outs, cuts):
        out[...] = rows[:, low:high]
    if extra:
        total = sums[0][...] + part1[count:, :] + part2[count:, :] + part3[count:, :]
        for i in range(3):
            outs[-1][8 * i : 8 * i + 8, :] = total[:, 128 * i : 128 * i + 128]


def tiny_body(part, down_o, first_o, second_o, head_o):
    rows = turned(part[...])
    rank = down_o.shape[0]
    down_o[...] = rows[0:rank]
    for i, out in enumerate((first_o, second_o, head_o)):
        out[...] = rows[rank + i : rank + i + 1, 0 : out.shape[1]]


def seq_pairs(move):
    pairs = []
    for source in range(32):
        z, x, core = source // 8, (source // 2) % 4, source % 2
        z, x, core = move(z, x, core)
        pairs.append((source, ((z % 4) * 4 + x % 4) * 2 + core % 2))
    return pairs


def swap_core(array):
    return lax.ppermute(array, "seq", seq_pairs(lambda z, x, c: (z, x, c + 1)))


def move_x(array, d):
    return lax.ppermute(array, "seq", seq_pairs(lambda z, x, c: (z, x + d, c)))


def move_z(array, d):
    return lax.ppermute(array, "seq", seq_pairs(lambda z, x, c: (z + d, x, c)))


def move_y(array, d):
    return lax.ppermute(array, "head", [(s, (s + d) % 4) for s in range(4)])


def move_first(array, d):
    return lax.ppermute(
        array, "seq", seq_pairs(lambda z, x, c: (z, x + d, c) if c == 0 else (z + d, x, c))
    )


def move_second(array, d):
    return lax.ppermute(
        array, "seq", seq_pairs(lambda z, x, c: (z + d, x, c) if c == 0 else (z, x + d, c))
    )


def start_scatter(keep, other, name, extra):
    size, cols = (keep.shape[0] - 8 * extra) // 4, keep.shape[1]
    half, tail = size // 2, 8 * extra
    rows = [size, size, half + tail, half + tail, size] + [8] * extra
    return kernel_call(
        functools.partial(part_body, extra),
        [shape(n, cols) for n in rows],
        name + "_part",
        False,
        scalars=0,
        limit=8,
    )(keep, other)


def relay_scatter(parts, up_in, down_in, name, extra):
    own, one, _, _, three, *sums = parts
    size, cols = own.shape
    return kernel_call(
        functools.partial(relay_body, extra),
        [shape(size + 8 * extra, cols), shape(size, cols)] + [shape(8, cols)] * extra,
        name + "_relay",
        False,
        scalars=0,
        limit=8,
    )(one, three, up_in, down_in, *sums)


def fine_scatter(own, relayed, name, extra):
    one, three, *sums = relayed
    size, cols = own.shape
    fine = size // 4
    return kernel_call(
        functools.partial(fine_body, extra),
        [shape(fine, cols)] + [shape(fine + 8 * extra, cols)] * 3 + [shape(8, cols)] * extra,
        name + "_fine",
        False,
        scalars=0,
        limit=8,
    )(own, move_first(one, 1), move_first(three, -1), *sums)


def end_scatter(fines, name, cuts, extra):
    fine, cols = fines[0].shape
    outs = [shape(fine, high - low) for low, high in cuts] + [shape(24, HEAD_K)] * extra
    return kernel_call(
        functools.partial(end_body, extra, cuts), outs, name + "_end", False, scalars=0, limit=8
    )(fines[0], *[move_second(fines[d], d) for d in (1, 2, 3)], *fines[4:])


def exchange(array):
    return lax.all_to_all(array, "head", 0, 0, tiled=True)


def gather_y(array):
    return [array] + [move_y(array, d) for d in (1, 2, 3)]


def on_device(
    tokens,
    first_gain,
    query_weight,
    key_weight,
    value_weight,
    outgate_weight,
    decay_down,
    decay_up,
    decay_bias,
    head_gain,
    output_weight,
    second_gain,
    mlp_gate,
    mlp_up,
    mlp_down,
    cotangent,
):
    place = lax.axis_index("seq")
    head = lax.axis_index("head")
    z, x, core = place // 8, (place // 2) % 4, place % 2
    ids = jnp.stack([head, core, x, z]).astype(jnp.int32)
    rows, width = tokens.shape
    quarter = rows // 4
    hidden_width = mlp_gate.shape[1]
    first_row, second_row, head_row, bias_row = (
        a.astype(f32).reshape(1, -1) for a in (first_gain, second_gain, head_gain, decay_bias)
    )

    packed = [shape(HEAD_V // 2 + 8, HEAD_K)] * 2
    normed_one, mixer_rows, keep, send = kernel_call(
        first_body,
        [shape(rows, width, dtype=bf16), shape(rows, 512)] + packed,
        "first",
        False,
        limit=8,
        far=range(3, 8),
    )(ids, first_row, bias_row, tokens, key_weight, value_weight, decay_down.T, decay_up)

    near, kept, score = kernel_call(
        inner_body,
        [shape(rows, 640), shape(rows, 896), shape(rows, rows)],
        "inner",
        True,
        far=range(1, 7),
        away=(1, 2),
        scalars=0,
        limit=8,
    )(bias_row, normed_one, mixer_rows, query_weight, outgate_weight, decay_down.T, decay_up)
    start_halves, (chip, row) = scan_states(ids, keep, send, False, near)
    half = output_weight.shape[0] // 2
    my_half = lax.dynamic_slice_in_dim(output_weight, core * half, half, 0).astype(f32)
    my_half = after(my_half, chip)
    from_one, from_three = move_y(my_half, 1), move_y(my_half, -1)
    upper, lower = kernel_call(
        forward_body, [shape(half // 2, width)] * 2, "forward", False, scalars=0
    )(*after((from_one, from_three), row))
    from_two = move_y(upper, 1), move_y(lower, -1)

    mixed, gated, start_state = kernel_call(
        gated_body,
        [shape(rows, HEAD_V), shape(rows, HEAD_V), shape(HEAD_V, HEAD_K)],
        "gated",
        False,
    )(ids, head_row, near, *start_halves)
    all_gated = gather_y(gated)
    from_heads = kernel_call(
        bundle_body, [shape(3, half, width)], "bundle", False, scalars=0
    )(*after((from_one, *from_two, from_three), gated))[0]
    out_weights = kernel_call(
        heads_body, [shape(4, *output_weight.shape, dtype=bf16)], "heads", False
    )(ids, output_weight, from_heads, swap_core(from_heads))[0]
    order = jnp.arange(width)
    to_core = (core + (order >> 9)) % 2
    one, two = (order >> 7) & 3, (order >> 5) & 3
    to_x = (x + jnp.where(to_core == 0, one, two)) % 4
    to_z = (z + jnp.where(to_core == 0, two, one)) % 4
    source = to_z * 256 + to_x * 64 + to_core * 32 + (order & 31)
    select = (jnp.arange(width)[:, None] == source[None, :]).astype(bf16)
    grad_hidden = mm(cotangent, mlp_down, NT)
    cot_sent = jnp.dot(cotangent, select)
    normed_one_sent = jnp.dot(normed_one, select)

    wide = [shape(rows, hidden_width, dtype=bf16)] * 3
    (
        middle, normed_two, hidden, grad_gate_act, grad_up_act, *parts,
    ) = kernel_call(
        feed_body,
        [shape(rows, width), shape(rows, width, dtype=bf16)] + wide + [shape(quarter, width)] * 4,
        "feed",
        False,
        away=(1, 2, 3, 4),
        limit=8,
        scratch=[(rows, width)],
    )(ids, second_row, tokens, *all_gated, out_weights, mlp_gate.T, mlp_up.T, grad_hidden)
    parts = [parts[0]] + [move_y(parts[d], d) for d in (1, 2, 3)]
    normed_two_sent = jnp.dot(normed_two, select)
    hidden_later = after(hidden, parts[1])
    keep_one, send_one = kernel_call(
        weights_one_body,
        [shape(width // 2, -(-3 * hidden_width // 128) * 128)] * 2,
        "weights_one",
        False,
        scalars=0,
        limit=20,
        far=range(5),
        away=(0, 1),
    )(normed_two_sent, cot_sent, hidden_later, grad_gate_act, grad_up_act)
    other_one = swap_core(send_one)
    ffn_part = jnp.dot(hidden, mlp_down, preferred_element_type=f32)
    parts[0] = after(parts[0], keep_one, ffn_part)

    grad_middle, second_sum, *grad_heads = kernel_call(
        middle_body,
        [shape(quarter, width), shape(1, width)] + [shape(quarter, HEAD_V)] * 4,
        "middle",
        True,
        limit=8,
    )(ids, second_row, middle, cotangent, out_weights, *parts)
    grad_heads = [grad_heads[0]] + [move_y(grad_heads[d], -d) for d in (1, 2, 3)]

    parts_one = list(start_scatter(keep_one, other_one, "one", 0))
    grad_heads[0] = after(grad_heads[0], parts_one[0])
    grad_mixed, grad_outgate, head_sum, keep, send = kernel_call(
        mixed_body,
        [
            shape(rows, HEAD_V),
            shape(rows, HEAD_V, dtype=bf16),
            shape(1, HEAD_V),
            shape(HEAD_V // 2 + 8, HEAD_K),
            shape(HEAD_V // 2 + 8, HEAD_K),
        ],
        "mixed",
        False,
        away=(0, 1, 2),
        limit=8,
        scratch=[(rows, HEAD_V)],
    )(ids, head_row, *grad_heads, mixed, near, mixer_rows)

    grad_query, back, early = kernel_call(
        inner_back_body,
        [shape(rows, HEAD_K, dtype=bf16), shape(rows, 512), shape(rows, width)],
        "inner_back",
        True,
        far=range(8),
        away=(0, 1, 2),
        scalars=0,
        limit=8,
    )(
        grad_mixed, mixer_rows, kept, score, start_state, grad_outgate, outgate_weight,
        query_weight,
    )
    grad_middle_all = lax.all_gather(after(grad_middle, keep), "head", tiled=True)
    ffn_sum = lax.psum(after(ffn_part, back), "head")
    output = kernel_call(
        add_body,
        [shape(rows, width)],
        "output",
        False,
        scalars=0,
        far=(0, 1),
        away=(0,),
        work=2 * 10**10,
    )(middle, ffn_sum)[0]

    end_halves, (_, row) = scan_states(ids, keep, send, True, early)
    up_one, down_one = after((parts_one[2], parts_one[3]), row)
    up_one, down_one = move_first(up_one, 1), move_first(down_one, -1)
    early = after(early, up_one, down_one)

    grad_key_value, packet, small, parts = kernel_call(
        outer_back_body,
        [shape(rows, 384, dtype=bf16), shape(8, width), shape(24, HEAD_K), shape(rows, width)],
        "outer_back",
        False,
        limit=16,
        far=range(3, 13),
        late=(7, 8, 9, 11, 12),
        away=(0, 2),
    )(
        ids, *end_halves, start_state, mixer_rows, kept, back, early, key_weight, value_weight,
        decay_up, decay_down.T, tokens, second_sum, head_sum,
    )
    packets = gather_y(packet)
    parts = exchange(parts)
    grad_rows = kernel_call(last_body, [shape(rows, width)], "last", False)(
        ids, first_row, tokens, grad_middle, parts
    )[0]
    grad_tokens = exchange(grad_rows)

    parts_one[1] = after(parts_one[1], small)
    relayed_one = relay_scatter(parts_one, up_one, down_one, "one", 0)
    packets[0] = after(packets[0], relayed_one[0])
    keep_two, send_two = kernel_call(
        weights_two_body,
        [shape(width // 2 + 8, 1152)] * 2,
        "weights_two",
        False,
        scalars=0,
        limit=20,
        far=range(7),
        away=(0, 1),
    )(
        normed_one_sent, grad_query, grad_key_value, grad_outgate, grad_middle_all, gated,
        select, source[None, :], *packets, small,
    )
    other_two = swap_core(send_two)
    parts_two = start_scatter(keep_two, other_two, "two", 1)
    parts_two = list(parts_two)
    parts_two[0], parts_two[1] = after(parts_two[0], grad_rows), after(parts_two[1], parts)
    up_two, down_two = move_first(parts_two[2], 1), move_first(parts_two[3], -1)
    relayed_two = relay_scatter(parts_two, up_two, down_two, "two", 1)
    fine_one = fine_scatter(after(parts_one[0], relayed_two[1]), relayed_one, "one", 0)
    fine_two = fine_scatter(parts_two[0], relayed_two, "two", 1)
    (
        grad_query_w, grad_key_w, grad_value_w, grad_outgate_w, grad_output_w, tiny, small,
    ) = end_scatter(
        fine_two, "two", ((0, 128), (128, 256), (256, 512), (512, 768), (768, 1024), (1024, 1152)), 1
    )
    fine_one = [after(fine_one[0], fine_two[0]), *fine_one[1:]]
    grad_gate, grad_up, grad_down = end_scatter(
        fine_one,
        "one",
        (
            (0, hidden_width),
            (hidden_width, 2 * hidden_width),
            (2 * hidden_width, 3 * hidden_width),
        ),
        0,
    )
    grad_down_w, grad_first, grad_second, grad_head = kernel_call(
        tiny_body,
        [shape(decay_down.shape[1], 32), shape(1, 32), shape(1, 32), shape(1, HEAD_V // 32)],
        "tiny",
        False,
        scalars=0,
        limit=2,
    )(tiny)
    return (
        output,
        grad_tokens,
        grad_first[0],
        grad_query_w,
        grad_key_w,
        grad_value_w,
        grad_outgate_w,
        grad_down_w.T,
        small[0:16],
        small[16],
        grad_head[0],
        grad_output_w.T,
        grad_second[0],
        grad_gate,
        grad_up,
        grad_down.T,
    )


def solution(mesh):
    placed = (
        P("seq", None),
        P(),
        P(None, "head"),
        P(None, "head"),
        P(None, "head"),
        P(None, "head"),
        P(),
        P(None, "head"),
        P("head"),
        P(),
        P("head", None),
        P(),
        P(None, "head"),
        P(None, "head"),
        P("head", None),
        P("seq", None),
    )
    return jax.shard_map(
        on_device,
        mesh=mesh,
        in_specs=placed,
        out_specs=(
            P("seq", None),
            P("seq", None),
            P("seq"),
            P("seq", "head"),
            P("seq", "head"),
            P("seq", "head"),
            P("seq", "head"),
            P("seq", None),
            P(None, "head"),
            P("head"),
            P("seq"),
            P("head", "seq"),
            P("seq"),
            P("seq", "head"),
            P("seq", "head"),
            P("head", "seq"),
        ),
        check_vma=False,
    )
```

```python
import functools

import jax
import jax.numpy as jnp
from jax import lax
from jax.experimental import pallas as pl
from jax.experimental.pallas import tpu as pltpu
from jax.sharding import PartitionSpec as P

HEAD_K = 128
HEAD_V = 256
epsilon = 1e-05
decay_norm = 16.0
key_scale = HEAD_K ** (-0.5)
f32 = jnp.float32
bf16 = jnp.bfloat16
highest = lax.Precision.HIGHEST

NN = (((1,), (0,)), ((), ()))
NT = (((1,), (1,)), ((), ()))
TN = (((0,), (0,)), ((), ()))


def mm(a, b, dims=NN):
    return lax.dot_general(a, b, dims, preferred_element_type=f32)


def mmh(a, b, dims=NN):
    return lax.dot_general(a, b, dims, precision=highest, preferred_element_type=f32)


def shape(*dims, dtype=f32):
    return jax.ShapeDtypeStruct(dims, dtype)


def kernel_call(body, outs, name, shade, scalars=1, limit=8, scratch=(), far=(), away=(), late=(), work=1):
    def run(*args):
        count, results = len(args), len(outs)

        def whole(*refs):
            refs = list(refs)
            sems = refs.pop()
            held = refs[count + results + len(scratch) :]
            ins, results_refs = refs[:count], refs[count : count + results]
            copies, writes = [], []
            for i in far:
                copies.append(pltpu.make_async_copy(ins[i], held[len(copies)], sems.at[len(copies)]))
                copies[-1].start()
                ins[i] = held[len(copies) - 1]
            for i in away:
                at = len(far) + len(writes)
                writes.append(pltpu.make_async_copy(held[at], results_refs[i], sems.at[at]))
                results_refs[i] = held[at]
            for i, copy in zip(far, copies):
                if i not in late:
                    copy.wait()
            given = [dict(zip(far, copies))] if late else []
            own = refs[count + results : count + results + len(scratch)]
            body(*given, *ins, *results_refs, *own)
            for write in writes:
                write.start()
            for write in writes:
                write.wait()

        specs = []
        for i in range(count):
            space = pltpu.SMEM if i < scalars else pltpu.HBM if i in far else pltpu.VMEM
            specs.append(pl.BlockSpec(memory_space=space))
        out_specs = [
            pl.BlockSpec(memory_space=pltpu.HBM if i in away else pltpu.VMEM)
            for i in range(results)
        ]
        scratches = [pltpu.VMEM(dims, f32) for dims in scratch]
        scratches += [pltpu.VMEM(args[i].shape, args[i].dtype) for i in far]
        scratches += [pltpu.VMEM(outs[i].shape, outs[i].dtype) for i in away]
        scratches.append(pltpu.SemaphoreType.DMA((max(1, len(far) + len(away)),)))
        args = [
            pltpu.with_memory_space_constraint(a, pltpu.HBM) if i in far else a
            for i, a in enumerate(args)
        ]
        return pl.pallas_call(
            whole,
            out_shape=[
                pltpu.HBM(o.shape, o.dtype) if i in away else o for i, o in enumerate(outs)
            ],
            in_specs=specs,
            out_specs=out_specs,
            scratch_shapes=scratches,
            name=name,
            compiler_params=pltpu.CompilerParams(vmem_limit_bytes=limit * 1024 * 1024),
            cost_estimate=pl.CostEstimate(
                flops=10**13 if shade else work,
                bytes_accessed=sum(a.size * a.dtype.itemsize for a in [*args, *outs]) if shade else 1,
                transcendentals=0,
            ),
        )(*args)

    return run


def after(value, *earlier):
    return lax.optimization_barrier((value, earlier))[0]


def pieces(array):
    one = array.astype(bf16)
    rest = array - one.astype(f32)
    two = rest.astype(bf16)
    return one, two, (rest - two.astype(f32)).astype(bf16)


def mm_exact(left, right, dims=NN):
    count = right.shape[1]
    out = mm(left, jnp.concatenate(pieces(right), axis=1), dims)
    return out[:, 0:count] + out[:, count : 2 * count] + out[:, 2 * count :]


def rms_scale(array):
    return lax.rsqrt(jnp.mean(array * array, axis=-1, keepdims=True) + epsilon)


def norm_back(grad_normed, unit_rows, gain_row, factor):
    scaled = grad_normed * gain_row
    return factor * (scaled - unit_rows * jnp.mean(scaled * unit_rows, axis=-1, keepdims=True))


def logistic(v):
    return 1.0 / (1.0 + jnp.exp(-v))


def pair_ids(rows):
    return (
        lax.broadcasted_iota(jnp.int32, (rows, rows), 0),
        lax.broadcasted_iota(jnp.int32, (rows, rows), 1),
    )


def level_steps(rows):
    return [1 << k for k in range(rows.bit_length() - 1)]


def odd_rows(step, rows):
    return (lax.broadcasted_iota(jnp.int32, (rows, 1), 0) & step) != 0


def level_maps(rows):
    row_ids, col_ids = pair_ids(rows)
    apart = row_ids ^ col_ids
    lower = jnp.where(col_ids <= row_ids, apart, 2 * rows)
    upper = jnp.where(col_ids > row_ids, apart, 2 * rows)
    return lower, upper


def level_weight(step, decay_parts, maps):
    lower, upper = maps
    near = jnp.where(odd_rows(step, lower.shape[0]), lower, upper)
    picked = jnp.where(near < step, 1.0, 0.0).astype(bf16)
    count = decay_parts.shape[1] // 3
    out = mm(picked, decay_parts)
    return jnp.exp(out[:, 0:count] + out[:, count : 2 * count] + out[:, 2 * count :])


def level_mask(step, maps):
    return jnp.logical_and(maps[0] >= step, maps[0] < 2 * step)


def first_body(
    ids, gain, bias, tokens, key_w, value_w, down, up,
    normed_o, rows_o, keep_o, send_o,
):
    rows = tokens[...].astype(f32)
    normed = (rows * rms_scale(rows) * gain[...]).astype(bf16)
    normed_o[...] = normed
    key = mm(normed, key_w[...])
    value = mm(normed, value_w[...])
    logit = mmh(mm(normed, down[...], NT), up[...].astype(f32)) + bias[...]
    decay = (jnp.minimum(logit, 0.0) - jnp.log1p(jnp.exp(-jnp.abs(logit)))) / decay_norm
    rows_o[:, 0:128] = key
    rows_o[:, 128:384] = value
    rows_o[:, 384:512] = decay
    state = mmh(value, key * tail_weight(decay), TN)
    pack_state(ids[1], state, jnp.sum(decay, axis=0, keepdims=True), keep_o, send_o)


def tail_weight(decay):
    row_ids, col_ids = pair_ids(decay.shape[0])
    return jnp.exp(mm_exact(jnp.where(col_ids > row_ids, 1.0, 0.0).astype(bf16), decay))


def pack_state(core, state, total, keep_o, send_o):
    half = HEAD_V // 2
    first = core == 0
    keep_o[0:half, :] = jnp.where(first, state[0:half], state[half:])
    send_o[0:half, :] = jnp.where(first, state[half:], state[0:half])
    packed = jnp.broadcast_to(total, (8, HEAD_K))
    keep_o[half:, :] = packed
    send_o[half:, :] = packed


def split_rows_kvd(rows):
    return rows.at[:, 0:128], rows.at[:, 128:384], rows.at[:, 384:512]


def inner_body(
    bias, normed_r, rows_r, query_w, gate_w, down, up, near_o, kept_o, score_o,
):
    gate_o, inner_o, qexp_o = near_o.at[:, 0:256], near_o.at[:, 256:512], near_o.at[:, 512:640]
    query_o, grown_o, tail_o = (kept_o.at[:, 128 * i : 128 * i + 128] for i in range(3))
    keyt_o, state_o, slope_o, low_o = (kept_o.at[:, 128 * i : 128 * i + 128] for i in range(3, 7))
    key_r, value_r, decay_r = split_rows_kvd(rows_r)
    normed = normed_r[...]
    query = mm(normed, query_w[...])
    gate_o[...] = mm(normed, gate_w[...])
    query_o[...] = query
    key, value, decay = key_r[...], value_r[...], decay_r[...]
    low = mm(normed, down[...], NT)
    low_o[...] = jnp.concatenate([low, jnp.zeros((low.shape[0], 112), f32)], axis=1)
    logit = mmh(low, up[...].astype(f32)) + bias[...]
    slope_o[...] = logistic(-logit) / decay_norm
    tail = tail_weight(decay)
    tail_o[...] = tail
    key_tail = key * tail
    keyt_o[...] = key_tail
    state_o[...] = mmh(value, key_tail, TN)
    rows = query.shape[0]
    row_ids, col_ids = pair_ids(rows)
    picked = jnp.where(row_ids >= col_ids, 1.0, 0.0).astype(bf16)
    grown = jnp.exp(mm_exact(picked, decay)) * key_scale
    grown_o[...] = grown
    qexp_o[...] = query * grown
    half = rows // 2
    maps = level_maps(half)
    for at in (0, half):
        cut_q, cut_k, cut_d = (a[at : at + half] for a in (query, key, decay))
        parts = jnp.concatenate(pieces(cut_d), axis=1)
        score = jnp.where(maps[0] == 0, jnp.sum(cut_q * cut_k, axis=-1, keepdims=True), 0.0)
        for step in level_steps(half):
            weight = level_weight(step, parts, maps)
            odd = odd_rows(step, half)
            left = jnp.where(odd, cut_q * weight, 0.0)
            right = jnp.where(odd, 0.0, cut_k * weight)
            score = jnp.where(level_mask(step, maps), mmh(left, right, NT), score)
        score_o[at : at + half, at : at + half] = score * key_scale
    score_o[0:half, half:] = jnp.zeros((half, half), f32)
    left, right = half_weights(decay)
    score_o[half:, 0:half] = mmh(query[half:] * left, key[:half] * right, NT) * key_scale
    inner_o[...] = mmh(score_o[...], value)


def half_weights(decay):
    half = decay.shape[0] // 2
    row_ids, col_ids = pair_ids(half)
    upto = jnp.where(row_ids >= col_ids, 1.0, 0.0).astype(bf16)
    beyond = jnp.where(row_ids < col_ids, 1.0, 0.0).astype(bf16)
    return jnp.exp(mm_exact(upto, decay[half:])), jnp.exp(mm_exact(beyond, decay[:half]))


def forward_body(one, three, upper, lower):
    half = upper.shape[0]
    upper[...] = one[0:half, :]
    lower[...] = three[half:, :]


def bundle_body(one, upper, lower, three, out):
    half = upper.shape[0]
    out[0] = one[...]
    out[1, 0:half, :] = upper[...]
    out[1, half:, :] = lower[...]
    out[2] = three[...]


def heads_body(ids, own, mine, other, out):
    half = mine.shape[1]
    low = ids[1] == 0
    out[0] = own[...]
    for i in range(3):
        out[i + 1, 0:half, :] = jnp.where(low, mine[i], other[i]).astype(bf16)
        out[i + 1, half:, :] = jnp.where(low, other[i], mine[i]).astype(bf16)


def join_halves(core, mine, theirs):
    first = core == 0
    return jnp.concatenate(
        [jnp.where(first, mine, theirs), jnp.where(first, theirs, mine)], axis=0
    )


def gated_body(ids, gain, near, mine, theirs, mixed_o, gated_o, start_o):
    gate, inner, qexp = near.at[:, 0:256], near.at[:, 256:512], near.at[:, 512:640]
    start = join_halves(ids[1], mine[...], theirs[...])
    start_o[...] = start
    mixed = inner[...] + mmh(qexp[...], start, NT)
    mixed_o[...] = mixed
    unit = mixed * rms_scale(mixed)
    gate_rows = gate[...]
    swish = gate_rows * logistic(gate_rows)
    gated_o[...] = (unit * gain[...] * swish).astype(bf16).astype(f32)


def split_rows(head, array, outs):
    count = array.shape[0] // 4
    for i, out in enumerate(outs):
        place = lax.rem(head + i, 4)
        out[...] = array[pl.ds(pl.multiple_of(place * count, count), count), :]


def feed_body(
    ids, gain, tokens, gated0, gated1, gated2, gated3, out_w, gate_w, up_w, grad_hidden,
    middle_o, normed_o, hidden_o, ggate_o, gup_o, part0, part1, part2, part3, total,
):
    middle = tokens[...].astype(f32)
    for i, gated in enumerate((gated0, gated1, gated2, gated3)):
        middle = middle + mm(gated[...].astype(bf16), out_w[i])
    middle_o[...] = middle
    normed = (middle * rms_scale(middle) * gain[...]).astype(bf16)
    normed_o[...] = normed
    gate = mm(normed, gate_w[...], NT)
    up = mm(normed, up_w[...], NT)
    sig = logistic(gate)
    swish = gate * sig
    hidden_o[...] = (swish * up).astype(bf16)
    grad = grad_hidden[...]
    grad_gate = (grad * up * (sig * (1.0 + gate * (1.0 - sig)))).astype(bf16)
    grad_up = (grad * swish).astype(bf16)
    ggate_o[...] = grad_gate
    gup_o[...] = grad_up
    total[...] = mm(grad_gate, gate_w[...]) + mm(grad_up, up_w[...])
    split_rows(ids[0], total, (part0, part1, part2, part3))


def middle_body(
    ids, gain, middle, cot, out_w, part0, part1, part2, part3,
    grad_o, sum_o, gated0, gated1, gated2, gated3,
):
    count = grad_o.shape[0]
    place = pl.ds(pl.multiple_of(ids[0] * count, count), count)
    rows = middle[place, :]
    factor = rms_scale(rows)
    unit = rows * factor
    grad = part0[...] + part1[...] + part2[...] + part3[...]
    sum_o[...] = jnp.sum(grad * unit, axis=0, keepdims=True)
    grad_middle = cot[place, :].astype(f32) + norm_back(grad, unit, gain[...], factor)
    grad_o[...] = grad_middle
    low = grad_middle.astype(bf16)
    for i, out in enumerate((gated0, gated1, gated2, gated3)):
        out[...] = mm(low, out_w[i], NT)


def sum_quarters(parts):
    count = parts.shape[0] // 4
    return (
        parts[0:count, :]
        + parts[count : 2 * count, :]
        + parts[2 * count : 3 * count, :]
        + parts[3 * count :, :]
    )


def mixed_body(
    ids, gain_r, part0, part1, part2, part3, mixed_r, near, rows,
    gmix_o, gout_o, sum_o, keep_o, send_o, total,
):
    gate_r, qexp = near.at[:, 0:256], near.at[:, 512:640]
    decay = rows.at[:, 384:512]
    count = part0.shape[0]
    for i, part in enumerate((part0, part1, part2, part3)):
        place = lax.rem(ids[0] + i, 4)
        total[pl.ds(pl.multiple_of(place * count, count), count), :] = part[...]
    grad = total[...]
    mixed = mixed_r[...]
    factor = rms_scale(mixed)
    unit = mixed * factor
    gain = gain_r[...]
    gate = gate_r[...]
    sig = logistic(gate)
    swish = gate * sig
    slope = sig * (1.0 + gate * (1.0 - sig))
    gout_o[...] = (grad * unit * gain * slope).astype(bf16)
    inward = grad * swish
    sum_o[...] = jnp.sum(inward * unit, axis=0, keepdims=True)
    gmix = norm_back(inward, unit, gain, factor)
    gmix_o[...] = gmix
    state = mmh(gmix, qexp[...], TN)
    pack_state(ids[1], state, jnp.sum(decay[...], axis=0, keepdims=True), keep_o, send_o)


def inner_back_body(
    gmix_r, rows_r, kept, score, start, gout, gate_w, query_w, gquery_o, back_o, early_o,
):
    query_r, grown = kept.at[:, 0:128], kept.at[:, 128:256]
    key_r, value_r, decay_r = split_rows_kvd(rows_r)
    both_o, gkey_o, gvalue_o = back_o.at[:, 0:128], back_o.at[:, 128:256], back_o.at[:, 256:512]
    gmix = gmix_r[...]
    query, key, decay = query_r[...], key_r[...], decay_r[...]
    rows = query.shape[0]
    pair = mmh(gmix, value_r[...], NT) * key_scale
    gvalue_o[...] = mmh(score[...], gmix, TN)
    half = rows // 2
    maps = level_maps(half)
    left, right = half_weights(decay)
    low_pair = pair[half:, 0:half]
    far_q = left * mmh(low_pair, key[:half] * right)
    far_k = right * mmh(low_pair, query[half:] * left, TN)
    from_start = grown[...] * mmh(gmix, start[...])
    all_q, all_k = [], []
    for at in (0, half):
        cut_q, cut_k, cut_d = (a[at : at + half] for a in (query, key, decay))
        cut_pair = pair[at : at + half, at : at + half]
        parts = jnp.concatenate(pieces(cut_d), axis=1)
        same = jnp.sum(jnp.where(maps[0] == 0, cut_pair, 0.0), axis=-1, keepdims=True)
        gq, gk = same * cut_k, same * cut_q
        for step in level_steps(half):
            weight = level_weight(step, parts, maps)
            odd = odd_rows(step, half)
            left = jnp.where(odd, cut_q * weight, 0.0)
            right = jnp.where(odd, 0.0, cut_k * weight)
            inside = jnp.where(level_mask(step, maps), cut_pair, 0.0)
            gq = gq + weight * mmh(inside, right)
            gk = gk + weight * mmh(inside, left, TN)
        all_q.append(gq)
        all_k.append(gk)
    gquery = from_start + jnp.concatenate([all_q[0], all_q[1] + far_q], axis=0)
    gkey = jnp.concatenate([all_k[0] + far_k, all_k[1]], axis=0)
    both_o[...] = query * gquery
    low = gquery.astype(bf16)
    gquery_o[...] = low
    gkey_o[...] = gkey
    early_o[...] = mm(gout[...], gate_w[...], NT) + mm(low, query_w[...], NT)


def outer_back_body(
    copies, ids, mine, theirs, start, rows_r, kept, back, early, key_w, value_w, up, down, tokens,
    second_sum, head_sum, gkv_o, packet_o, small_o, total,
):
    tail, key_tail, state, slope, low = (
        kept.at[:, 128 * i : 128 * i + 128] for i in range(2, 7)
    )
    key_r, value_r, decay_r = split_rows_kvd(rows_r)
    both, gkey_r, gvalue_r = back.at[:, 0:128], back.at[:, 128:256], back.at[:, 256:512]
    end = join_halves(ids[1], mine[...], theirs[...])
    key = key_r[...]
    gkey = gkey_r[...] + tail[...] * mmh(value_r[...], end)
    gvalue = gvalue_r[...] + mmh(key_tail[...], end, NT)
    whole = jnp.exp(jnp.sum(decay_r[...], axis=0, keepdims=True))
    later = jnp.sum((whole * start[...] + state[...]) * end, axis=0, keepdims=True)
    row_ids, col_ids = pair_ids(key.shape[0])
    picked = jnp.where(col_ids >= row_ids, 1.0, 0.0).astype(bf16)
    gdecay = mm_exact(picked, both[...] - key * gkey) + later
    glogit = gdecay * slope[...]
    glow = mmh(glogit, up[...].astype(f32), NT)
    turned_low = mmh(up[...].astype(f32), glogit, NT)
    for i in range(4):
        packet_o[i : i + 1, :] = jnp.concatenate(
            [turned_low[4 * i + j : 4 * i + j + 1, :] for j in range(4)], axis=1
        )
    small_o[0:16, :] = mmh(low[:, 0:16], glogit, TN)
    small_o[16:24, :] = jnp.broadcast_to(jnp.sum(glogit, axis=0, keepdims=True), (8, HEAD_K))
    gkey_low = gkey.astype(bf16)
    gvalue_low = gvalue.astype(bf16)
    gkv_o[:, 0:128] = gkey_low
    gkv_o[:, 128:384] = gvalue_low
    for i in (7, 8, 9, 11, 12):
        copies[i].wait()
    grad = early[...] + mm(gkey_low, key_w[...], NT) + mm(gvalue_low, value_w[...], NT)
    grad = grad + mmh(glow, down[...].astype(f32))
    rows = tokens[...].astype(f32)
    packet_o[4:5, :] = jnp.sum(grad * (rows * rms_scale(rows)), axis=0, keepdims=True)
    packet_o[5:6, :] = second_sum[...]
    packet_o[6:7, :] = jnp.concatenate(
        [head_sum[...], jnp.zeros((1, rows.shape[1] - HEAD_V), f32)], axis=1
    )
    packet_o[7:8, :] = jnp.zeros((1, rows.shape[1]), f32)
    total[...] = grad


def last_body(ids, gain, tokens, grad_middle, parts, out):
    count = grad_middle.shape[0]
    rows = tokens[pl.ds(pl.multiple_of(ids[0] * count, count), count), :].astype(f32)
    factor = rms_scale(rows)
    grad = parts[0:count, :] + parts[count : 2 * count, :] + parts[2 * count : 3 * count, :]
    grad = grad + parts[3 * count :, :]
    grad = grad_middle[...] + norm_back(grad, rows * factor, gain[...], factor)
    for i in range(4):
        out[i * count : (i + 1) * count, :] = grad


def add_body(left, right, out):
    out[...] = left[...] + right[...]


def weights_one_body(normed, cot, hidden, grad_gate, grad_up, keep_o, send_o):
    half = keep_o.shape[0]
    width = grad_gate.shape[1]
    for out, at in ((keep_o, 0), (send_o, half)):
        left = normed[:, at : at + half]
        out[:, 0:width] = mm(left, grad_gate[...], TN)
        out[:, width : 2 * width] = mm(left, grad_up[...], TN)
        tail = jnp.zeros((half, out.shape[1] - 3 * width), f32)
        down = mm(cot[:, at : at + half], hidden[...], TN)
        out[:, 2 * width :] = jnp.concatenate([down, tail], axis=1)


def weights_two_body(
    normed, gquery, gkv, gout, low, gated, select, source, packet0, packet1, packet2, packet3,
    small, keep_o, send_o,
):
    half = normed.shape[1] // 2
    low_sent = mm(low[...].astype(bf16), select[...]).astype(bf16)
    width = select.shape[0]
    packet = packet0[...] + packet1[...] + packet2[...] + packet3[...]
    count = normed.shape[0]
    turned_low = jnp.concatenate(
        [packet[i // 4 : i // 4 + 1, (i % 4) * count : (i % 4 + 1) * count] for i in range(16)],
        axis=0,
    )
    rank = turned_low.shape[0]
    glow_parts = jnp.concatenate(pieces(turned_low), axis=0)
    rows = jnp.concatenate([packet[4:6, :], jnp.zeros((6, width), f32)], axis=0)
    row_parts = jnp.concatenate(pieces(rows), axis=0)
    heads = jnp.concatenate(
        [jnp.zeros((2, HEAD_V), f32), packet[6:7, 0:HEAD_V], jnp.zeros((5, HEAD_V), f32)], axis=0
    )
    head_parts = jnp.concatenate(pieces(heads), axis=0)
    share = HEAD_V // 32
    for out, at in ((keep_o, 0), (send_o, half)):
        left = normed[:, at : at + half]
        out[half:, :] = jnp.concatenate(
            [small[0:8, :], small[8:16, :], small[16:24, :], jnp.zeros((8, 768), f32)], axis=1
        )
        out[0:half, 0:128] = mm(left, gquery[...], TN)
        out[0:half, 128:256] = mm(left, gkv[:, 0:128], TN)
        out[0:half, 256:512] = mm(left, gkv[:, 128:384], TN)
        out[0:half, 512:768] = mm(left, gout[...], TN)
        out[0:half, 768:1024] = mm(low_sent[:, at : at + half], gated[...].astype(bf16), TN)
        down = mm(left, glow_parts, (((0,), (1,)), ((), ())))
        from_feature = source[:, at : at + half]
        inside = from_feature & 31
        from_head = jnp.where(inside < share, (from_feature >> 5) * share + inside, -1)
        head_ids = lax.broadcasted_iota(jnp.int32, (HEAD_V, half), 0)
        spread = jnp.where(head_ids == from_head, 1.0, 0.0).astype(bf16)
        tail = mm(select[:, at : at + half], row_parts, (((0,), (1,)), ((), ())))
        tail = tail + mm(spread, head_parts, (((0,), (1,)), ((), ())))
        out[0:half, 1024:1152] = jnp.concatenate(
            [
                down[:, 0:rank] + down[:, rank : 2 * rank] + down[:, 2 * rank :],
                tail[:, 0:8] + tail[:, 8:16] + tail[:, 16:24],
                jnp.zeros((half, 104), f32),
            ],
            axis=1,
        )


def cut(packed):
    half = HEAD_V // 2
    return packed[0:half, :], packed[half : half + 1, :]


def pack(out, state, decay):
    half = HEAD_V // 2
    out[0:half, :] = state
    out[half:, :] = jnp.broadcast_to(decay, (8, HEAD_K))


def chip_body(reverse, ids, keep, other, first_o, chip_o):
    mine, theirs = keep[...], other[...]
    is_first = ids[1] == (1 if reverse else 0)
    first = jnp.where(is_first, mine, theirs)
    first_o[...] = first
    first_state, first_decay = cut(first)
    second_state, second_decay = cut(jnp.where(is_first, theirs, mine))
    pack(
        chip_o, jnp.exp(second_decay) * first_state + second_state, first_decay + second_decay
    )


def earlier(parts, place):
    state, decay = 0.0, jnp.zeros((1, HEAD_K), f32)
    for d in (1, 2, 3):
        part_state, part_decay = cut(parts[d - 1])
        held = place >= d
        state = state + jnp.where(held, jnp.exp(decay), 0.0) * part_state
        decay = decay + jnp.where(held, part_decay, 0.0)
    return state, decay


def line_body(reverse, ids, own, part1, part2, part3, row_o, whole_o):
    line = 3 - ids[2] if reverse else ids[2]
    parts = [own[...], part1[...], part2[...], part3[...]]
    pack(row_o, *earlier(parts[1:], line))
    whole = 0.0
    for d in range(4):
        decay = jnp.zeros((1, HEAD_K), f32)
        for e in range(4):
            if e != d:
                later = lax.rem(line + 4 - e, 4) > lax.rem(line + 4 - d, 4)
                decay = decay + jnp.where(later, cut(parts[e])[1], 0.0)
        whole = whole + jnp.exp(decay) * cut(parts[d])[0]
    pack(whole_o, whole, sum(cut(p)[1] for p in parts))


def plane_body(reverse, ids, part1, part2, part3, row, first, mine_o, theirs_o):
    deep = 3 - ids[3] if reverse else ids[3]
    plane_state, _ = earlier([part1[...], part2[...], part3[...]], deep)
    row_state, row_decay = cut(row[...])
    before = jnp.exp(row_decay) * plane_state + row_state
    first_state, first_decay = cut(first[...])
    past = jnp.exp(first_decay) * before + first_state
    is_first = ids[1] == (1 if reverse else 0)
    mine_o[...] = jnp.where(is_first, before, past)
    theirs_o[...] = jnp.where(is_first, past, before)


def scan_states(ids, keep, send, reverse, beside, beside_line=None):
    sign = -1 if reverse else 1
    side = "later" if reverse else "earlier"
    packed = [shape(HEAD_V // 2 + 8, HEAD_K)] * 2
    other = swap_core(send)
    first, chip = kernel_call(
        functools.partial(chip_body, reverse), packed, "chip_" + side, False, limit=2
    )(ids, keep, other)
    from_x = [move_x(chip, sign * d) for d in (1, 2, 3)]
    line_chip = chip if beside_line is None else after(chip, beside_line)
    row, whole = kernel_call(
        functools.partial(line_body, reverse), packed, "line_" + side, False, limit=2
    )(ids, line_chip, *from_x)
    extra = (chip, row)
    row = after(row, beside)
    mine, theirs = kernel_call(
        functools.partial(plane_body, reverse),
        [shape(HEAD_V // 2, HEAD_K)] * 2,
        "plane_" + side,
        False,
        limit=2,
    )(ids, *[move_z(whole, sign * d) for d in (1, 2, 3)], row, first)
    return (mine, swap_core(theirs)), extra


def part_body(extra, keep, other, own, one, up, down, three, *sums):
    size = own.shape[0]
    half = size // 2
    for out, at in ((own, 0), (one, size), (up, 2 * size), (down, 2 * size + half), (three, 3 * size)):
        count = min(out.shape[0], half) if out is up or out is down else size
        out[0:count, :] = keep[at : at + count, :] + other[at : at + count, :]
    if extra:
        total = keep[4 * size :, :] + other[4 * size :, :]
        up[half:, :] = total
        down[half:, :] = total
        sums[0][...] = total


def relay_body(extra, one, three, up, down, *rest):
    size = three.shape[0]
    half = size // 2
    sums, to_one, to_three = rest[:extra], rest[extra], rest[extra + 1]
    to_one[0:half, :] = one[0:half, :] + up[0:half, :]
    to_one[half:size, :] = one[half:, :]
    to_three[0:half, :] = three[0:half, :]
    to_three[half:, :] = three[half:, :] + down[0:half, :]
    if extra:
        to_one[size:, :] = up[half:, :]
        rest[extra + 2][...] = sums[0][...] + up[half:, :] + down[half:, :]


def fine_body(extra, own, up, down, *rest):
    sums, outs = rest[:extra], rest[extra:]
    count = outs[0].shape[0]
    total = None
    if extra:
        total = sums[0][...] + up[4 * count :, :]
        outs[4][...] = total
    for d in range(4):
        rows = slice(d * count, (d + 1) * count)
        outs[d][0:count, :] = own[rows, :] + up[rows, :] + down[rows, :]
        if extra and d > 0:
            outs[d][count:, :] = total


def turned(array):
    count = array.shape[0]
    row_ids, col_ids = pair_ids(count)
    same = jnp.where(row_ids == col_ids, 1.0, 0.0)
    return mmh(array, same, TN)


def end_body(extra, cuts, part0, part1, part2, part3, *rest):
    sums, outs = rest[:extra], rest[extra:]
    count = part0.shape[0]
    rows = part0[...] + part1[0:count, :] + part2[0:count, :] + part3[0:count, :]
    for out, (low, high) in zip(outs, cuts):
        out[...] = rows[:, low:high]
    if extra:
        total = sums[0][...] + part1[count:, :] + part2[count:, :] + part3[count:, :]
        for i in range(3):
            outs[-1][8 * i : 8 * i + 8, :] = total[:, 128 * i : 128 * i + 128]


def tiny_body(part, down_o, first_o, second_o, head_o):
    rows = turned(part[...])
    rank = down_o.shape[0]
    down_o[...] = rows[0:rank]
    for i, out in enumerate((first_o, second_o, head_o)):
        out[...] = rows[rank + i : rank + i + 1, 0 : out.shape[1]]


def seq_pairs(move):
    pairs = []
    for source in range(32):
        z, x, core = source // 8, (source // 2) % 4, source % 2
        z, x, core = move(z, x, core)
        pairs.append((source, ((z % 4) * 4 + x % 4) * 2 + core % 2))
    return pairs


def swap_core(array):
    return lax.ppermute(array, "seq", seq_pairs(lambda z, x, c: (z, x, c + 1)))


def move_x(array, d):
    return lax.ppermute(array, "seq", seq_pairs(lambda z, x, c: (z, x + d, c)))


def move_z(array, d):
    return lax.ppermute(array, "seq", seq_pairs(lambda z, x, c: (z + d, x, c)))


def move_y(array, d):
    return lax.ppermute(array, "head", [(s, (s + d) % 4) for s in range(4)])


def move_first(array, d):
    return lax.ppermute(
        array, "seq", seq_pairs(lambda z, x, c: (z, x + d, c) if c == 0 else (z + d, x, c))
    )


def move_second(array, d):
    return lax.ppermute(
        array, "seq", seq_pairs(lambda z, x, c: (z + d, x, c) if c == 0 else (z, x + d, c))
    )


def start_scatter(keep, other, name, extra):
    size, cols = (keep.shape[0] - 8 * extra) // 4, keep.shape[1]
    half, tail = size // 2, 8 * extra
    rows = [size, size, half + tail, half + tail, size] + [8] * extra
    return kernel_call(
        functools.partial(part_body, extra),
        [shape(n, cols) for n in rows],
        name + "_part",
        False,
        scalars=0,
        limit=8,
    )(keep, other)


def relay_scatter(parts, up_in, down_in, name, extra):
    own, one, _, _, three, *sums = parts
    size, cols = own.shape
    return kernel_call(
        functools.partial(relay_body, extra),
        [shape(size + 8 * extra, cols), shape(size, cols)] + [shape(8, cols)] * extra,
        name + "_relay",
        False,
        scalars=0,
        limit=8,
    )(one, three, up_in, down_in, *sums)


def fine_scatter(own, relayed, name, extra):
    one, three, *sums = relayed
    size, cols = own.shape
    fine = size // 4
    return kernel_call(
        functools.partial(fine_body, extra),
        [shape(fine, cols)] + [shape(fine + 8 * extra, cols)] * 3 + [shape(8, cols)] * extra,
        name + "_fine",
        False,
        scalars=0,
        limit=8,
    )(own, move_first(one, 1), move_first(three, -1), *sums)


def end_scatter(fines, name, cuts, extra):
    fine, cols = fines[0].shape
    outs = [shape(fine, high - low) for low, high in cuts] + [shape(24, HEAD_K)] * extra
    return kernel_call(
        functools.partial(end_body, extra, cuts), outs, name + "_end", False, scalars=0, limit=8
    )(fines[0], *[move_second(fines[d], d) for d in (1, 2, 3)], *fines[4:])


def exchange(array):
    return lax.all_to_all(array, "head", 0, 0, tiled=True)


def gather_y(array):
    return [array] + [move_y(array, d) for d in (1, 2, 3)]


def on_device(
    tokens,
    first_gain,
    query_weight,
    key_weight,
    value_weight,
    outgate_weight,
    decay_down,
    decay_up,
    decay_bias,
    head_gain,
    output_weight,
    second_gain,
    mlp_gate,
    mlp_up,
    mlp_down,
    cotangent,
):
    place = lax.axis_index("seq")
    head = lax.axis_index("head")
    z, x, core = place // 8, (place // 2) % 4, place % 2
    ids = jnp.stack([head, core, x, z]).astype(jnp.int32)
    rows, width = tokens.shape
    quarter = rows // 4
    hidden_width = mlp_gate.shape[1]
    first_row, second_row, head_row, bias_row = (
        a.astype(f32).reshape(1, -1) for a in (first_gain, second_gain, head_gain, decay_bias)
    )

    packed = [shape(HEAD_V // 2 + 8, HEAD_K)] * 2
    normed_one, mixer_rows, keep, send = kernel_call(
        first_body,
        [shape(rows, width, dtype=bf16), shape(rows, 512)] + packed,
        "first",
        False,
        limit=8,
        far=range(3, 8),
    )(ids, first_row, bias_row, tokens, key_weight, value_weight, decay_down.T, decay_up)

    near, kept, score = kernel_call(
        inner_body,
        [shape(rows, 640), shape(rows, 896), shape(rows, rows)],
        "inner",
        True,
        far=range(3, 7),
        away=(1, 2),
        scalars=0,
        limit=8,
    )(bias_row, normed_one, mixer_rows, query_weight, outgate_weight, decay_down.T, decay_up)
    grad_hidden = mm(cotangent, mlp_down, NT)
    start_halves, (chip, row) = scan_states(ids, keep, send, False, near, grad_hidden)
    half = output_weight.shape[0] // 2
    my_half = lax.dynamic_slice_in_dim(output_weight, core * half, half, 0).astype(f32)
    my_half = after(my_half, chip)
    from_one, from_three = move_y(my_half, 1), move_y(my_half, -1)
    upper, lower = kernel_call(
        forward_body, [shape(half // 2, width)] * 2, "forward", False, scalars=0
    )(*after((from_one, from_three), row))
    from_two = move_y(upper, 1), move_y(lower, -1)

    mixed, gated, start_state = kernel_call(
        gated_body,
        [shape(rows, HEAD_V), shape(rows, HEAD_V), shape(HEAD_V, HEAD_K)],
        "gated",
        False,
        away=(2,),
    )(ids, head_row, near, *start_halves)
    all_gated = gather_y(gated)
    from_heads = kernel_call(
        bundle_body, [shape(3, half, width)], "bundle", False, scalars=0
    )(*after((from_one, *from_two, from_three), gated))[0]
    out_weights = kernel_call(
        heads_body, [shape(4, *output_weight.shape, dtype=bf16)], "heads", False
    )(ids, output_weight, from_heads, swap_core(from_heads))[0]
    order = jnp.arange(width)
    to_core = (core + (order >> 9)) % 2
    one, two = (order >> 7) & 3, (order >> 5) & 3
    to_x = (x + jnp.where(to_core == 0, one, two)) % 4
    to_z = (z + jnp.where(to_core == 0, two, one)) % 4
    source = to_z * 256 + to_x * 64 + to_core * 32 + (order & 31)
    select = (jnp.arange(width)[:, None] == source[None, :]).astype(bf16)
    cot_sent = jnp.dot(cotangent, select)
    normed_one_sent = jnp.dot(normed_one, select)

    all_gated[0] = after(all_gated[0], normed_one_sent)
    wide = [shape(rows, hidden_width, dtype=bf16)] * 3
    (
        middle, normed_two, hidden, grad_gate_act, grad_up_act, *parts,
    ) = kernel_call(
        feed_body,
        [shape(rows, width), shape(rows, width, dtype=bf16)] + wide + [shape(quarter, width)] * 4,
        "feed",
        False,
        away=(1, 2, 3, 4),
        limit=8,
        scratch=[(rows, width)],
    )(ids, second_row, tokens, *all_gated, out_weights, mlp_gate.T, mlp_up.T, grad_hidden)
    parts = [parts[0]] + [move_y(parts[d], d) for d in (1, 2, 3)]
    normed_two_sent = jnp.dot(normed_two, select)
    hidden_later = after(hidden, parts[1])
    keep_one, send_one = kernel_call(
        weights_one_body,
        [shape(width // 2, -(-3 * hidden_width // 128) * 128)] * 2,
        "weights_one",
        False,
        scalars=0,
        limit=20,
        far=range(5),
        away=(0, 1),
    )(normed_two_sent, cot_sent, hidden_later, grad_gate_act, grad_up_act)
    other_one = swap_core(send_one)
    ffn_part = jnp.dot(hidden, mlp_down, preferred_element_type=f32)
    parts[0] = after(parts[0], keep_one, ffn_part)

    grad_middle, second_sum, *grad_heads = kernel_call(
        middle_body,
        [shape(quarter, width), shape(1, width)] + [shape(quarter, HEAD_V)] * 4,
        "middle",
        True,
        limit=8,
    )(ids, second_row, middle, cotangent, out_weights, *parts)
    grad_heads = [grad_heads[0]] + [move_y(grad_heads[d], -d) for d in (1, 2, 3)]

    parts_one = list(start_scatter(keep_one, other_one, "one", 0))
    grad_heads[0] = after(grad_heads[0], parts_one[0])
    grad_mixed, grad_outgate, head_sum, keep, send = kernel_call(
        mixed_body,
        [
            shape(rows, HEAD_V),
            shape(rows, HEAD_V, dtype=bf16),
            shape(1, HEAD_V),
            shape(HEAD_V // 2 + 8, HEAD_K),
            shape(HEAD_V // 2 + 8, HEAD_K),
        ],
        "mixed",
        False,
        away=(0, 1, 2),
        limit=8,
        scratch=[(rows, HEAD_V)],
    )(ids, head_row, *grad_heads, mixed, near, mixer_rows)

    grad_query, back, early = kernel_call(
        inner_back_body,
        [shape(rows, HEAD_K, dtype=bf16), shape(rows, 512), shape(rows, width)],
        "inner_back",
        True,
        far=range(8),
        away=(0, 1, 2),
        scalars=0,
        limit=8,
    )(
        grad_mixed, mixer_rows, kept, score, start_state, grad_outgate, outgate_weight,
        query_weight,
    )
    grad_middle_all = lax.all_gather(after(grad_middle, keep), "head", tiled=True)
    ffn_sum = lax.psum(after(ffn_part, back), "head")
    output = kernel_call(
        add_body,
        [shape(rows, width)],
        "output",
        False,
        scalars=0,
        far=(0, 1),
        away=(0,),
        work=2 * 10**10,
    )(middle, ffn_sum)[0]

    end_halves, (_, row) = scan_states(ids, keep, send, True, early)
    up_one, down_one = after((parts_one[2], parts_one[3]), row)
    up_one, down_one = move_first(up_one, 1), move_first(down_one, -1)
    early = after(early, up_one, down_one)

    grad_key_value, packet, small, parts = kernel_call(
        outer_back_body,
        [shape(rows, 384, dtype=bf16), shape(8, width), shape(24, HEAD_K), shape(rows, width)],
        "outer_back",
        False,
        limit=16,
        far=range(3, 13),
        late=(7, 8, 9, 11, 12),
        away=(0, 2),
    )(
        ids, *end_halves, start_state, mixer_rows, kept, back, early, key_weight, value_weight,
        decay_up, decay_down.T, tokens, second_sum, head_sum,
    )
    packets = gather_y(packet)
    parts = exchange(parts)
    grad_rows = kernel_call(last_body, [shape(rows, width)], "last", False)(
        ids, first_row, tokens, grad_middle, parts
    )[0]
    grad_tokens = exchange(grad_rows)

    parts_one[1] = after(parts_one[1], small)
    relayed_one = relay_scatter(parts_one, up_one, down_one, "one", 0)
    packets[0] = after(packets[0], relayed_one[0])
    keep_two, send_two = kernel_call(
        weights_two_body,
        [shape(width // 2 + 8, 1152)] * 2,
        "weights_two",
        False,
        scalars=0,
        limit=20,
        far=range(7),
        away=(0, 1),
    )(
        normed_one_sent, grad_query, grad_key_value, grad_outgate, grad_middle_all, gated,
        select, source[None, :], *packets, small,
    )
    other_two = swap_core(send_two)
    parts_two = start_scatter(keep_two, other_two, "two", 1)
    parts_two = list(parts_two)
    parts_two[0], parts_two[1] = after(parts_two[0], grad_rows), after(parts_two[1], parts)
    up_two, down_two = move_first(parts_two[2], 1), move_first(parts_two[3], -1)
    relayed_two = relay_scatter(parts_two, up_two, down_two, "two", 1)
    fine_one = fine_scatter(after(parts_one[0], relayed_two[1]), relayed_one, "one", 0)
    fine_two = fine_scatter(parts_two[0], relayed_two, "two", 1)
    (
        grad_query_w, grad_key_w, grad_value_w, grad_outgate_w, grad_output_w, tiny, small,
    ) = end_scatter(
        fine_two, "two", ((0, 128), (128, 256), (256, 512), (512, 768), (768, 1024), (1024, 1152)), 1
    )
    fine_one = [after(fine_one[0], fine_two[0]), *fine_one[1:]]
    grad_gate, grad_up, grad_down = end_scatter(
        fine_one,
        "one",
        (
            (0, hidden_width),
            (hidden_width, 2 * hidden_width),
            (2 * hidden_width, 3 * hidden_width),
        ),
        0,
    )
    grad_down_w, grad_first, grad_second, grad_head = kernel_call(
        tiny_body,
        [shape(decay_down.shape[1], 32), shape(1, 32), shape(1, 32), shape(1, HEAD_V // 32)],
        "tiny",
        False,
        scalars=0,
        limit=2,
    )(tiny)
    return (
        output,
        grad_tokens,
        grad_first[0],
        grad_query_w,
        grad_key_w,
        grad_value_w,
        grad_outgate_w,
        grad_down_w.T,
        small[0:16],
        small[16],
        grad_head[0],
        grad_output_w.T,
        grad_second[0],
        grad_gate,
        grad_up,
        grad_down.T,
    )


def solution(mesh):
    placed = (
        P("seq", None),
        P(),
        P(None, "head"),
        P(None, "head"),
        P(None, "head"),
        P(None, "head"),
        P(),
        P(None, "head"),
        P("head"),
        P(),
        P("head", None),
        P(),
        P(None, "head"),
        P(None, "head"),
        P("head", None),
        P("seq", None),
    )
    return jax.shard_map(
        on_device,
        mesh=mesh,
        in_specs=placed,
        out_specs=(
            P("seq", None),
            P("seq", None),
            P("seq"),
            P("seq", "head"),
            P("seq", "head"),
            P("seq", "head"),
            P("seq", "head"),
            P("seq", None),
            P(None, "head"),
            P("head"),
            P("seq"),
            P("head", "seq"),
            P("seq"),
            P("seq", "head"),
            P("seq", "head"),
            P("head", "seq"),
        ),
        check_vma=False,
    )
```
